128 devices in a mesh: wave: 16 (over z, x_hi, core), lev: 8 (over y, x_lo).
Axes of the slice: x: 4 (x_hi: 2, x_lo: 2; x = x_hi * 2 + x_lo), y: 4, z: 4, core: 2. Of those that a mesh axis runs over, the one named last changes fastest.
Arguments:
- spectra: float32 [320, 136, 2, 384], P('wave', 'lev'), may hold values from -6 to 6
- band_filter: float32 [4, 384], replicated, may hold values from 0.5 to 2
- band_blocks: int32 [4, 12], replicated, may hold values 0 or 1
- legendre: float32 [320, 384, 640], P('wave'), may hold values from -0.3125 to 0.3125
- vert_cov: float32 [4, 32, 136, 136], P(None, 'wave'), may hold values from -0.5 to 0.5
- lat_cov: int32 [640], replicated, may hold values from 0 to 31
Outputs:
- result: float32 [320, 136, 2, 384], P('wave', 'lev')
The draws below stay inside these ranges and needn't reach their ends.
All inputs are finite; a program needn't handle non-finite values.
Results may differ from the reference program's by a relative error of at most 0.000071.
Values sent between devices are 32-bit elements; how exact they have to be, the bound alone decides.
A program may use at most 256 MiB of HBM per device.

```python
import math
import jax
import jax.numpy as jnp
from jax import lax

M = 320
N = 384
LEV = 136
BANDS = 4
BLKN = 32
NCOV = 32
LAT = 640
NBLK = 12


def set_ends(result, own_key, smallest, high):
    spot = [jax.random.randint(jax.random.fold_in(own_key, axis), (), 0, length) for axis, length in enumerate(result.shape)]
    longest = result.shape.index(max(result.shape))
    neighbour = spot[:longest] + [(spot[longest] + 1) % result.shape[longest]] + spot[longest + 1:]
    return result.at[tuple(spot)].set(smallest).at[tuple(neighbour)].set(high)


def block_levels(stream_key, dims, shards, least, top_value):
    def one(axis_at, blocks):
        draws = jax.random.uniform(jax.random.fold_in(jax.random.fold_in(stream_key, 6), axis_at), (blocks,), jnp.float32, least / len(shards), top_value / len(shards))
        return jnp.repeat(jnp.exp(draws), dims[axis_at] // blocks).reshape((-1,) + (1,) * (len(dims) - axis_at - 1))

    level = one(*shards[0])
    for cut in shards[1:]:
        level = level * one(*cut)
    return level


def bell_draw(own_key, extent, width, reach, shards=(), held_as=jnp.bfloat16):
    values = jax.random.normal(own_key, extent, jnp.float32) * width
    if len(shards) > 0:
        values = block_levels(own_key, extent, shards, -0.22, 0.18) * values
    return jnp.clip(values, min=-reach, max=reach).astype(held_as)


def setup_inputs(seed: int = 0) -> dict:
    seeds = jax.random.split(jax.random.key(seed), 7)
    return {
        "spectra": bell_draw(seeds[0], (M, LEV, 2, N), 1.0, 6.0, ((0, 16), (1, 8)), jnp.float32),
        "band_filter": jnp.clip(jnp.exp(jax.random.uniform(seeds[1], (BANDS, N), jnp.float32, math.log(0.5), math.log(2.0))), 0.5, 2.0),
        "band_blocks": set_ends((jax.random.randint(seeds[2], (BANDS, NBLK), 0, 4) < 3).astype(jnp.int32), jax.random.fold_in(seeds[2], 1), 0, 1),
        "legendre": bell_draw(seeds[3], (M, N, LAT), N ** -0.5, 0.3125, ((0, 16),), jnp.float32),
        "vert_cov": bell_draw(seeds[4], (BANDS, NCOV, LEV, LEV), LEV ** -0.5, 0.5, ((1, 16),), jnp.float32),
        "lat_cov": set_ends(jax.random.randint(seeds[5], (LAT,), 0, NCOV), jax.random.fold_in(seeds[5], 1), 0, NCOV - 1).astype(jnp.int32),
    }


def reference(spectra, band_filter, band_blocks, legendre, vert_cov, lat_cov):
    waves = jnp.arange(N, dtype=jnp.int32)
    zonal = jnp.arange(M, dtype=jnp.int32)
    triangle = (waves[None, :] >= zonal[:, None]).astype(jnp.float32)
    filters = band_filter * jnp.repeat(band_blocks.astype(jnp.float32), BLKN, axis=1)
    selected = jnp.take(vert_cov, lat_cov, axis=1)

    def per_wave(items):
        field, table, row_mask = items
        weights = (filters * row_mask[None, :])[:, None, None, :]
        filtered = (field[None] * weights).reshape(BANDS * LEV * 2, N)
        gridded = jnp.dot(filtered, table, precision=lax.Precision.HIGHEST).reshape(BANDS, LEV, 2, LAT)
        covaried = jnp.einsum("bpkl,blrp->bkrp", selected, gridded, precision=lax.Precision.HIGHEST)
        adjoint_out = jnp.dot(covaried.reshape(BANDS * LEV * 2, LAT), table.T, precision=lax.Precision.HIGHEST)
        return jnp.sum(adjoint_out.reshape(BANDS, LEV, 2, N) * weights, axis=0)

    return lax.map(per_wave, (spectra, legendre, triangle))
```

```python
import functools
import jax, jax.numpy as jnp
from jax import lax
from jax.experimental import pallas as pl
from jax.experimental.pallas import tpu as pltpu

F32, BF = jnp.float32, jnp.bfloat16
HALF_BLOCK = 544
BLOCK = 1248

NT = (((1,), (1,)), ((), ()))

def split(x):
    hi = x.astype(BF)
    lo = (x - hi.astype(F32)).astype(BF)
    return hi, lo

def dot_nt(a, b):
    return lax.dot_general(a, b, NT, preferred_element_type=F32)

def k2(starts, rank, w, wt, s_ref, l_hbm, cov_hbm, out_ref,
       lbuf, cov, perm, a_cat, lp_cat, s_cat, g, cv, wcol, lsem, csem, *, phases=4):
    lev = lax.axis_index("lev")
    o = lax.rem(lev, 2)
    m0 = 5 * (lev // 2) + 2 * o
    first = lax.axis_index("wave") * 20 + m0
    lcopy = pltpu.make_async_copy(l_hbm.at[pl.ds(m0, 3)], lbuf, lsem)
    lcopy.start()
    ccopy = pltpu.make_async_copy(cov_hbm, cov, csem)
    ccopy.start()
    for t in range(5):
        row = lax.broadcasted_iota(jnp.int32, (128, 640), 0) + 128 * t
        perm[128 * t:128 * (t + 1), :] = (rank[...] == row).astype(F32).astype(BF)
    for b in range(4):
        wcol[:, 128 * b:128 * (b + 1)] = jnp.broadcast_to(wt[:, b:b + 1], (384, 128))
    lane = lax.broadcasted_iota(jnp.int32, (384, 128), 1)
    wtail = jnp.zeros((384, 128), F32)
    for b in range(4):
        wtail = jnp.where((lane >= 8 * b) & (lane < 8 * b + 8), wcol[:, 128 * b:128 * (b + 1)], wtail)
    wcol[:, 512:640] = wtail
    lcopy.wait()

    def prep(mi, _):
        hi, lo = split(lbuf[mi])
        p = perm[...]
        ahi = dot_nt(p, hi).astype(BF)
        a_cat[mi, :, 0:384] = ahi
        a_cat[mi, :, 384:768] = ahi
        a_cat[mi, :, 768:1152] = dot_nt(p, lo).astype(BF)
        lhi = dot_nt(hi, p).astype(BF)
        lp_cat[mi, :, 0:640] = lhi
        lp_cat[mi, :, 640:1280] = lhi
        lp_cat[mi, :, 1280:1920] = dot_nt(lo, p).astype(BF)
        return 0

    lax.fori_loop(0, 3, prep, 0)

    for s in range(5):
        mi = (s + o) // 2
        tri = (lax.broadcasted_iota(jnp.int32, (1, 384), 1) >= first + mi).astype(F32)
        rows = [s_ref[j, 17 * s:17 * s + 17, :] for j in range(8)]
        full = jnp.concatenate(rows, axis=0)
        for b in range(4):
            wb = w[b:b + 1, :] * tri
            hi, lo = split(full[0:128] * wb)
            s_cat[128 * b:128 * (b + 1), 0:384] = hi
            s_cat[128 * b:128 * (b + 1), 384:768] = lo
            s_cat[128 * b:128 * (b + 1), 768:1152] = hi
        tails = jnp.concatenate([full[128:136] * (w[b:b + 1, :] * tri) for b in range(4)], axis=0)
        tails = jnp.concatenate([tails, tails, tails, jnp.zeros_like(tails)], axis=0)
        hi, lo = split(tails)
        s_cat[512:640, 0:384] = hi
        s_cat[512:640, 384:768] = lo
        s_cat[512:640, 768:1152] = hi

        def fwd(t, _):
            off = pl.multiple_of(t * 128, 128)
            g[s, 0:640, pl.ds(off, 128)] = dot_nt(a_cat[mi], s_cat[pl.ds(off, 128), :])
            return 0
        lax.fori_loop(0, 5, fwd, 0)
        g[s, 640:672, :] = jnp.zeros((32, 640), F32)
    ccopy.wait()

    def covary(c, _):
        lo_row, hi_row = starts[c], starts[c + 1]
        base = (lo_row // 8) * 8
        lane128 = lax.broadcasted_iota(jnp.int32, (1, 128), 1)
        blk, odd = c // 2, lax.rem(c, 2)
        at = HALF_BLOCK * odd
        u = cov[blk, 1088:1224, :]
        group = lane128 // 32
        u = jnp.where(lax.rem(group, 2) == odd, u, pltpu.roll(u, 32, 1))
        u = jnp.concatenate([u[0:128], u[128:136], u[128:136], u[128:136], u[128:136]], axis=0)
        uhi, ulo = split(u)
        ucat = jnp.where(lane128 < 64, uhi.astype(F32), ulo.astype(F32))
        trow = cov[blk, pl.ds(pl.multiple_of(at + 512, 8), 32), :]

        def window(t, _):
            r0 = pl.multiple_of(base + 32 * t, 8)
            x = jnp.concatenate([g[s, pl.ds(r0, 32), :] for s in range(5)], axis=0)
            xhi, xlo = split(x)
            t_hi, t_lo = xhi[:, 512:640].astype(F32), xlo[:, 512:640].astype(F32)
            tcat = jnp.where((lane128 >= 32) & (lane128 < 64), t_lo, t_hi).astype(BF)
            row = r0 + lax.broadcasted_iota(jnp.int32, (32, 1), 0)
            keep = row >= lo_row
            tail_out = jnp.zeros((160, 32), F32)
            lane32 = lax.broadcasted_iota(jnp.int32, (1, 32), 1)
            for b in range(4):
                ub = jnp.where((lax.rem(lane128, 32) >= 8 * b) & (lax.rem(lane128, 32) < 8 * b + 8), ucat, 0.0).astype(BF)
                chi, clo = split(jnp.concatenate([cov[blk, pl.ds(pl.multiple_of(at + 128 * b, 8), 128), :], trow], axis=0))
                xb = xhi[:, 128 * b:128 * b + 128]
                lhs = jnp.concatenate([xb, xlo[:, 128 * b:128 * b + 128], xb, tcat], axis=1)
                rhs = jnp.concatenate([chi, chi, clo, ub], axis=1)
                res = dot_nt(lhs, rhs)
                for s in range(5):
                    old = cv[s, pl.ds(r0, 32), 128 * b:128 * b + 128]
                    cv[s, pl.ds(r0, 32), 128 * b:128 * b + 128] = jnp.where(keep, res[32 * s:32 * s + 32, 0:128], old)
                tail_out = jnp.where((lane32 >= 8 * b) & (lane32 < 8 * b + 8), res[:, 128:160], tail_out)
            for s in range(5):
                old = cv[s, pl.ds(r0, 32), 512:544]
                cv[s, pl.ds(r0, 32), 512:544] = jnp.where(keep, tail_out[32 * s:32 * s + 32], old)
            return 0

        lax.fori_loop(0, (hi_row - base + 31) // 32, window, 0)
        return 0

    for s in range(5):
        cv[s, :, 512:640] = jnp.zeros((672, 128), F32)
    if phases >= 3:
        lax.fori_loop(0, 32, covary, 0)

    if phases >= 4:
      for s in range(5):
        mi = (s + o) // 2
        acc = None
        for b in range(5):
            hi, lo = split(cv[s, 0:640, 128 * b:128 * b + 128])
            rhs = jnp.concatenate([hi, lo, hi], axis=0)
            part = jnp.dot(lp_cat[mi], rhs, preferred_element_type=F32)
            part = part * wcol[:, 128 * b:128 * b + 128]
            if b < 4:
                acc = part if acc is None else acc + part
            else:
                tail = part
        tail = tail + pltpu.roll(tail, 128 - 16, 1)
        tail = tail + pltpu.roll(tail, 128 - 8, 1)
        n = lax.broadcasted_iota(jnp.int32, (384, 1), 0)
        tri = (n >= first + mi).astype(F32)
        main = (acc * tri).T
        tail = (tail * tri).T
        res = jnp.concatenate([main, tail[0:8]], axis=0)
        for j in range(8):
            out_ref[j, 17 * s:17 * s + 17, :] = res[17 * j:17 * j + 17]


def compute(starts, rank, w, wt, s, legendre, cov, phases=4):
    vm = lambda: pl.BlockSpec(memory_space=pltpu.VMEM)
    return pl.pallas_call(
        functools.partial(k2, phases=phases),
        out_shape=jax.ShapeDtypeStruct((8, 85, 384), F32),
        in_specs=[pl.BlockSpec(memory_space=pltpu.SMEM), vm(), vm(), vm(), vm(),
                  pl.BlockSpec(memory_space=pl.ANY), pl.BlockSpec(memory_space=pl.ANY)],
        out_specs=vm(),
        scratch_shapes=[
            pltpu.VMEM((3, 384, 640), F32),
            pltpu.VMEM((16, BLOCK, 128), F32),
            pltpu.VMEM((640, 640), BF),
            pltpu.VMEM((3, 640, 1152), BF),
            pltpu.VMEM((3, 384, 1920), BF),
            pltpu.VMEM((640, 1152), BF),
            pltpu.VMEM((5, 672, 640), F32),
            pltpu.VMEM((5, 672, 640), F32),
            pltpu.VMEM((384, 640), F32),
            pltpu.SemaphoreType.DMA(()),
            pltpu.SemaphoreType.DMA(()),
        ],
        compiler_params=pltpu.CompilerParams(vmem_limit_bytes=61 * 2**20),
    )(starts, rank, w, wt, s, legendre, cov)


def pack_cov(vc):
    t = jnp.transpose(vc, (1, 0, 2, 3))
    main = t[:, :, :128, :128].reshape(2, 512, 128)
    rows = t[:, :, 128:, :128].reshape(2, 32, 128)
    u = jnp.transpose(t[:, :, :, 128:], (2, 0, 1, 3)).reshape(136, 64)
    u = jnp.concatenate([u, u], axis=1)
    top = jnp.concatenate([main, rows], axis=1).reshape(2 * HALF_BLOCK, 128)
    return jnp.concatenate([top, u, jnp.zeros((BLOCK - 1224, 128), F32)], axis=0)


def order(lat_cov):
    lat = lat_cov.astype(jnp.int32)
    p = jnp.arange(640, dtype=jnp.int32)
    before = (lat[:, None] < lat[None, :]) | ((lat[:, None] == lat[None, :]) & (p[:, None] < p[None, :]))
    rank = jnp.sum(before.astype(jnp.int32), axis=0)[None, :]
    starts = jnp.sum((lat[:, None] < jnp.arange(40, dtype=jnp.int32)[None, :]).astype(jnp.int32), axis=0)
    return rank, starts
QUARTER = BLOCK // 4
HALF = BLOCK // 2


def place():
    wave, lev = lax.axis_index("wave"), lax.axis_index("lev")
    return wave // 4, lax.rem(wave // 2, 2), lax.rem(wave, 2), lev // 2, lax.rem(lev, 2)


def at(z, xh, core, y, xl):
    return {"wave": (z * 2 + xh) * 2 + core, "lev": y * 2 + xl}


def greet(peers):
    barrier = pltpu.get_barrier_semaphore()
    for peer in peers:
        pl.semaphore_signal(barrier, inc=1, device_id=peer, device_id_type=pl.DeviceIdType.MESH)
    pl.semaphore_wait(barrier, len(peers))


def exchange_starts(src, dst, send, recv):
    me = lax.axis_index("lev")
    copies = []
    for step in (4, 3, 5, 2, 6, 1, 7):
        to = lax.rem(me + step, 8)
        copies.append(pltpu.make_async_remote_copy(
            src_ref=src.at[to], dst_ref=dst.at[me], send_sem=send.at[step - 1], recv_sem=recv.at[step - 1],
            device_id={"lev": to}, device_id_type=pl.DeviceIdType.MESH))
    return copies


def lev_peers():
    me = lax.axis_index("lev")
    return [{"lev": lax.rem(me + step, 8)} for step in range(1, 8)]


def gather_kernel(spec_ref, own_ref, s_out, cov_out, a_send, a_recv, c_send, c_recv, l_sem):
    z, xh, core, y, xl = place()
    me = lax.axis_index("lev")
    zu, zd, z2 = lax.rem(z + 1, 4), lax.rem(z + 3, 4), lax.rem(z + 2, 4)
    yu, yd, y2 = lax.rem(y + 1, 4), lax.rem(y + 3, 4), lax.rem(y + 2, 4)
    up, down = at(zu, xh, core, y, xl), at(zd, xh, core, y, xl)
    cross = at(z, 1 - xh, core, y, 1 - xl)
    yup, ydown = at(z, xh, core, yu, xl), at(z, xh, core, yd, xl)
    twin = at(z, xh, 1 - core, y, xl)
    greet(lev_peers() + [up, down, cross, twin])

    def block(zz, xx, kk=None):
        return (zz * 2 + xx) * 2 + (core if kk is None else kk)

    own = block(z, xh)
    ids = {}
    started = []

    def piece(blk, row, count):
        return cov_out.at[blk, pl.ds(pl.multiple_of(row, 8), count)]

    def send(name, target, blk, row, count, src=None):
        n = ids.setdefault(name, len(ids))
        ref = piece(blk, row, count)
        copy = pltpu.make_async_remote_copy(
            src_ref=ref if src is None else src.at[pl.ds(pl.multiple_of(row, 8), count)], dst_ref=ref,
            send_sem=c_send.at[n], recv_sem=c_recv.at[n], device_id=target, device_id_type=pl.DeviceIdType.MESH)
        copy.start()
        started.append(copy)

    def arrived(name, blk, row, count):
        n = ids[name]
        ref = piece(blk, row, count)
        pltpu.make_async_remote_copy(
            src_ref=ref, dst_ref=ref, send_sem=c_send.at[n], recv_sem=c_recv.at[n],
            device_id=twin, device_id_type=pl.DeviceIdType.MESH).wait_recv()

    swaps = exchange_starts(spec_ref, s_out, a_send, a_recv)
    for copy in swaps:
        copy.start()
    locals_ = [pltpu.make_async_copy(spec_ref.at[me], s_out.at[me], l_sem.at[0]),
               pltpu.make_async_copy(own_ref, cov_out.at[own], l_sem.at[1])]
    for copy in locals_:
        copy.start()
    send("x0", cross, own, QUARTER * y, QUARTER, own_ref)
    send("u0", up, own, 0, HALF, own_ref)
    send("d1", down, own, HALF, HALF, own_ref)
    send("u1", up, own, HALF, HALF, own_ref)
    send("d0", down, own, 0, HALF, own_ref)
    send("t0", twin, own, 0, BLOCK, own_ref)

    columns = (z, zd, zu, z2)

    def spread(n):
        blk = block(columns[n], 1 - xh)
        arrived(f"x{n}", blk, QUARTER * y, QUARTER)
        send(f"yu{n}", yup, blk, QUARTER * y, QUARTER)
        send(f"yd{n}", ydown, blk, QUARTER * y, QUARTER)

    def relay(n):
        blk = block(columns[n], 1 - xh)
        arrived(f"yu{n}", blk, QUARTER * yd, QUARTER)
        if n % 2 == 0:
            send(f"yf{n}", yup, blk, QUARTER * yd, QUARTER)
        arrived(f"yd{n}", blk, QUARTER * yu, QUARTER)
        if n % 2 == 1:
            send(f"yf{n}", ydown, blk, QUARTER * yu, QUARTER)

    def finish(n):
        blk = block(columns[n], 1 - xh)
        arrived(f"yf{n}", blk, QUARTER * y2, QUARTER)
        send(f"v{n}", twin, blk, 0, BLOCK)

    spread(0)
    arrived("u0", block(zd, xh), 0, HALF)
    send("uf", up, block(zd, xh), 0, HALF)
    arrived("d1", block(zu, xh), HALF, HALF)
    send("df", down, block(zu, xh), HALF, HALF)
    relay(0)
    arrived("u1", block(zd, xh), HALF, HALF)
    send("x1", cross, block(zd, xh), QUARTER * y, QUARTER)
    send("t1", twin, block(zd, xh), 0, BLOCK)
    arrived("d0", block(zu, xh), 0, HALF)
    send("x2", cross, block(zu, xh), QUARTER * y, QUARTER)
    send("t2", twin, block(zu, xh), 0, BLOCK)
    spread(1)
    spread(2)
    arrived("uf", block(z2, xh), 0, HALF)
    arrived("df", block(z2, xh), HALF, HALF)
    send("x3", cross, block(z2, xh), QUARTER * y, QUARTER)
    send("t3", twin, block(z2, xh), 0, BLOCK)
    finish(0)
    relay(1)
    relay(2)
    spread(3)
    finish(1)
    finish(2)
    relay(3)
    finish(3)
    for copy in locals_:
        copy.wait()
    for copy in swaps:
        copy.wait()
    for n in range(4):
        arrived(f"t{n}", block(columns[n], xh, 1 - core), 0, BLOCK)
        arrived(f"v{n}", block(columns[n], 1 - xh, 1 - core), 0, BLOCK)
    for copy in started:
        copy.wait_send()


def gather(spec, own):
    hbm = pl.BlockSpec(memory_space=pl.ANY)
    return pl.pallas_call(
        gather_kernel,
        out_shape=(jax.ShapeDtypeStruct(spec.shape, F32), jax.ShapeDtypeStruct((16, BLOCK, 128), F32)),
        in_specs=[hbm, hbm],
        out_specs=(hbm, hbm),
        scratch_shapes=[pltpu.SemaphoreType.DMA((7,)), pltpu.SemaphoreType.DMA((7,)),
                        pltpu.SemaphoreType.DMA((30,)), pltpu.SemaphoreType.DMA((30,)),
                        pltpu.SemaphoreType.DMA((2,))],
        compiler_params=pltpu.CompilerParams(collective_id=0, has_side_effects=True),
    )(spec, own)


def return_kernel(src, dst, a_send, a_recv, l_sem):
    me = lax.axis_index("lev")
    greet(lev_peers())
    swaps = exchange_starts(src, dst, a_send, a_recv)
    for copy in swaps:
        copy.start()
    own = pltpu.make_async_copy(src.at[me], dst.at[me], l_sem)
    own.start()
    own.wait()
    for copy in swaps:
        copy.wait()


def give_back(x):
    hbm = pl.BlockSpec(memory_space=pl.ANY)
    return pl.pallas_call(
        return_kernel,
        out_shape=jax.ShapeDtypeStruct(x.shape, F32),
        in_specs=[hbm],
        out_specs=hbm,
        scratch_shapes=[pltpu.SemaphoreType.DMA((7,)), pltpu.SemaphoreType.DMA((7,)), pltpu.SemaphoreType.DMA(())],
        compiler_params=pltpu.CompilerParams(collective_id=1, has_side_effects=True),
    )(x)


def local(spectra, band_filter, band_blocks, legendre, vert_cov, lat_cov):
    rank, starts = order(lat_cov)
    w = band_filter * jnp.repeat(band_blocks.astype(F32), 32, axis=1)
    wt = w.T
    packed = pack_cov(vert_cov)
    spec = jnp.transpose(spectra, (0, 2, 1, 3)).reshape(8, 85, 384)
    s, cov = gather(spec, packed)
    out = compute(starts, rank, w, wt, s, legendre, cov)
    back = give_back(out).reshape(20, 2, 17, 384)
    return jnp.transpose(back, (0, 2, 1, 3))


def solution(mesh):
    P = jax.sharding.PartitionSpec
    return jax.shard_map(
        local,
        mesh=mesh,
        in_specs=(P("wave", "lev", None, None), P(), P(), P("wave", None, None), P(None, "wave", None, None), P()),
        out_specs=P("wave", "lev", None, None),
        check_vma=False,
    )
```

```python
import functools
import jax
import jax.numpy as jnp
from jax import lax
from jax.experimental import pallas as pl
from jax.experimental.pallas import tpu as pltpu

F32, BF = jnp.float32, jnp.bfloat16
NT = (((1,), (1,)), ((), ()))
MESH = pl.DeviceIdType.MESH

HALF_BLOCK = 544
BLOCK = 1248
DIRECT = 480
REST = BLOCK - DIRECT
QUARTER = REST // 4


def split(x):
    hi = x.astype(BF)
    return hi, (x - hi.astype(F32)).astype(BF)


def dot_nt(a, b):
    return lax.dot_general(a, b, NT, preferred_element_type=F32)


def pack_cov(vc):
    t = jnp.transpose(vc, (1, 0, 2, 3))
    main = t[:, :, :128, :128].reshape(2, 512, 128)
    rows = t[:, :, 128:, :128].reshape(2, 32, 128)
    u = jnp.transpose(t[:, :, :, 128:], (2, 0, 1, 3)).reshape(136, 64)
    u = jnp.concatenate([u, u], axis=1)
    top = jnp.concatenate([main, rows], axis=1).reshape(2 * HALF_BLOCK, 128)
    return jnp.concatenate([top, u, jnp.zeros((BLOCK - 1224, 128), F32)], axis=0)


def place():
    wave, lev = lax.axis_index("wave"), lax.axis_index("lev")
    return wave // 4, lax.rem(wave // 2, 2), lax.rem(wave, 2), lev // 2, lax.rem(lev, 2)


def at(z, xh, core, y, xl):
    return {"wave": (z * 2 + xh) * 2 + core, "lev": y * 2 + xl}


def lev_peers():
    me = lax.axis_index("lev")
    return [{"lev": lax.rem(me + step, 8)} for step in range(1, 8)]


def greet(peers):
    barrier = pltpu.get_barrier_semaphore()
    for peer in peers:
        pl.semaphore_signal(barrier, inc=1, device_id=peer, device_id_type=MESH)


def met(peers):
    pl.semaphore_wait(pltpu.get_barrier_semaphore(), len(peers))


class Exchange:
    def __init__(self, src, dst, relay, send, recv):
        wave, me = lax.axis_index("wave"), lax.axis_index("lev")
        y, xl = me // 2, lax.rem(me, 2)

        def lev(dy, dx):
            return lax.rem(y + dy, 4) * 2 + (lax.rem(xl + dx, 2))

        def copy(n, source, target, to):
            return pltpu.make_async_remote_copy(
                src_ref=source, dst_ref=target, send_sem=send.at[n], recv_sem=recv.at[n],
                device_id={"wave": wave, "lev": to}, device_id_type=MESH)

        far = lev(2, 1)
        self.over = copy(0, src.at[far], relay, lev(3, 0))
        self.plain = [copy(1 + n, src.at[lev(dy, dx)], dst.at[me], lev(dy, dx))
                      for n, (dy, dx) in enumerate(((2, 0), (1, 1), (3, 1), (1, 0), (3, 0), (0, 1)))]
        self.on = copy(7, relay, dst.at[lev(1, 0)], lev(3, 1))

    def start(self):
        self.over.start()
        for c in self.plain:
            c.start()

    def hand_on(self):
        self.over.wait_recv()
        self.on.start()

    def finish(self):
        for c in self.plain:
            c.wait_recv()
        self.on.wait_recv()

    def sent(self):
        self.over.wait_send()
        for c in self.plain:
            c.wait_send()
        self.on.wait_send()


def part():
    lev = lax.axis_index("lev")
    o = lax.rem(lev, 2)
    m0 = 5 * (lev // 2) + 2 * o
    return m0, o, lax.axis_index("wave") * 20 + m0


def first_kernel(spec, own_ref, lat, w, leg, cov_out, g_out, lp_out,
                 s_in, relay, lbuf, perm, a_cat, lp, s_cat, g,
                 a_send, a_recv, c_send, c_recv, l_sem, o_sem):
    z, xh, core, y, xl = place()
    me = lax.axis_index("lev")
    zu, zd, z2 = lax.rem(z + 1, 4), lax.rem(z + 3, 4), lax.rem(z + 2, 4)
    yu, yd, y2 = lax.rem(y + 1, 4), lax.rem(y + 3, 4), lax.rem(y + 2, 4)
    up, down = at(zu, xh, core, y, xl), at(zd, xh, core, y, xl)
    cross = at(z, 1 - xh, core, y, 1 - xl)
    yup, ydown = at(z, xh, core, yu, xl), at(z, xh, core, yd, xl)
    twin = at(z, xh, 1 - core, y, xl)
    peers = lev_peers() + [up, down, cross, twin]
    m0, o, first = part()
    greet(peers)
    lcopy = pltpu.make_async_copy(leg.at[pl.ds(m0, 3)], lbuf, l_sem.at[0])
    lcopy.start()

    row = jnp.broadcast_to(lat[...], (8, 640)).astype(F32)
    column = row.T[:, 0:1]
    mine = row[0:1]
    p_row = lax.broadcasted_iota(jnp.int32, (1, 640), 1)
    rank = jnp.zeros((1, 640), F32)
    for t in range(5):
        c = column[128 * t:128 * t + 128]
        p_col = lax.broadcasted_iota(jnp.int32, (128, 1), 0) + 128 * t
        ahead = (c < mine) | ((c == mine) & (p_col < p_row))
        rank = rank + jnp.sum(ahead.astype(F32), axis=0, keepdims=True)
    for t in range(5):
        place_ = (lax.broadcasted_iota(jnp.int32, (128, 640), 0) + 128 * t).astype(F32)
        perm[128 * t:128 * t + 128, :] = (rank == place_).astype(F32).astype(BF)

    def block(zz, xx, kk=None):
        return (zz * 2 + xx) * 2 + (core if kk is None else kk)

    own = block(z, xh)
    columns = (z, zd, zu, z2)
    O = [block(c, xh) for c in columns]
    X = [block(c, 1 - xh) for c in columns]
    ids, started = {}, []

    def piece(blk, row, count):
        return cov_out.at[blk, pl.ds(pl.multiple_of(row, 8), count)]

    def send(name, target, blk, row, count, src=None):
        n = ids.setdefault(name, len(ids))
        ref = piece(blk, row, count)
        copy = pltpu.make_async_remote_copy(
            src_ref=ref if src is None else src.at[pl.ds(pl.multiple_of(row, 8), count)], dst_ref=ref,
            send_sem=c_send.at[n], recv_sem=c_recv.at[n], device_id=target, device_id_type=MESH)
        copy.start()
        started.append(copy)

    def arrived(name, blk, row, count):
        n = ids[name]
        ref = piece(blk, row, count)
        pltpu.make_async_remote_copy(
            src_ref=ref, dst_ref=ref, send_sem=c_send.at[n], recv_sem=c_recv.at[n],
            device_id=twin, device_id_type=MESH).wait_recv()

    def quarter(n):
        return DIRECT + QUARTER * n

    swap = Exchange(spec, s_in, relay, a_send, a_recv)

    def begin():
        met(peers)
        swap.start()
        send("xs", cross, own, quarter(y), QUARTER, own_ref)
        send("uD", up, own, 0, DIRECT, own_ref)
        send("dD", down, own, 0, DIRECT, own_ref)
        send("t0", twin, own, 0, BLOCK, own_ref)
        for copy in locals_:
            copy.start()

    locals_ = [pltpu.make_async_copy(spec.at[me], s_in.at[me], l_sem.at[1]),
               pltpu.make_async_copy(own_ref, cov_out.at[own], l_sem.at[2])]

    def y_sends(n):
        send(f"yu{n}", yup, X[n], quarter(y), QUARTER)
        send(f"yd{n}", ydown, X[n], quarter(y), QUARTER)

    def step1():
        swap.hand_on()
        send("xD0", cross, own, 0, DIRECT, own_ref)
        arrived("xs", X[0], quarter(y), QUARTER)
        send("us", up, X[0], quarter(y), QUARTER)
        send("ds", down, X[0], quarter(y), QUARTER)
        send("uR", up, own, DIRECT, REST, own_ref)
        send("dR", down, own, DIRECT, REST, own_ref)
        y_sends(0)

    def step2():
        arrived("uD", O[1], 0, DIRECT)
        send("uDf", up, O[1], 0, DIRECT // 2)
        send("xD1", cross, O[1], 0, DIRECT)
        arrived("dD", O[2], 0, DIRECT)
        send("dDf", down, O[2], DIRECT // 2, DIRECT // 2)
        send("xD2", cross, O[2], 0, DIRECT)
        arrived("us", X[1], quarter(y), QUARTER)
        send("usf", up, X[1], quarter(y), QUARTER // 2)
        arrived("ds", X[2], quarter(y), QUARTER)
        send("dsf", down, X[2], quarter(y) + QUARTER // 2, QUARTER // 2)
        y_sends(1)
        y_sends(2)

    def y_relay(n):
        arrived(f"yd{n}", X[n], quarter(yu), QUARTER)
        send(f"yf{n}", ydown, X[n], quarter(yu), QUARTER)

    def step3():
        arrived("uDf", O[3], 0, DIRECT // 2)
        arrived("dDf", O[3], DIRECT // 2, DIRECT // 2)
        send("xD3", cross, O[3], 0, DIRECT)
        arrived("usf", X[3], quarter(y), QUARTER // 2)
        arrived("dsf", X[3], quarter(y) + QUARTER // 2, QUARTER // 2)
        y_sends(3)
        y_relay(0)

    def step4():
        y_relay(1)
        y_relay(2)

    def step5():
        arrived("uR", O[1], DIRECT, REST)
        send("uRf", up, O[1], DIRECT, REST // 2)
        arrived("dR", O[2], DIRECT, REST)
        send("dRf", down, O[2], DIRECT + REST // 2, REST // 2)
        send("t1", twin, O[1], 0, BLOCK)
        send("t2", twin, O[2], 0, BLOCK)
        y_relay(3)

    def whole(n):
        arrived(f"xD{n}", X[n], 0, DIRECT)
        arrived(f"yu{n}", X[n], quarter(yd), QUARTER)
        arrived(f"yf{n}", X[n], quarter(y2), QUARTER)
        send(f"v{n}", twin, X[n], 0, BLOCK)

    def step9():
        arrived("uRf", O[3], DIRECT, REST // 2)
        arrived("dRf", O[3], DIRECT + REST // 2, REST // 2)
        send("t3", twin, O[3], 0, BLOCK)
        whole(3)

    outs = []

    def out(src, dst, n):
        copy = pltpu.make_async_copy(src, dst, o_sem.at[n])
        copy.start()
        outs.append(copy)

    def prep_a(mi):
        hi, lo = split(lbuf[mi])
        p = perm[...]
        ahi = dot_nt(p, hi).astype(BF)
        a_cat[mi, :, 0:384] = ahi
        a_cat[mi, :, 384:768] = ahi
        a_cat[mi, :, 768:1152] = dot_nt(p, lo).astype(BF)

    def prep_b(mi):
        hi, lo = split(lbuf[mi])
        p = perm[...]
        lp[mi, :, 0:640] = dot_nt(hi, p).astype(BF)
        lp[mi, :, 640:1280] = dot_nt(lo, p).astype(BF)
        out(lp.at[mi], lp_out.at[mi], mi)

    def synth(s):
        mi = (s + o) // 2
        tri = (lax.broadcasted_iota(jnp.int32, (1, 384), 1) >= first + mi).astype(F32)
        full = jnp.concatenate([s_in[j, 17 * s:17 * s + 17, :] for j in range(8)], axis=0)
        for b in range(4):
            hi, lo = split(full[0:128] * (w[b:b + 1, :] * tri))
            s_cat[128 * b:128 * (b + 1), 0:384] = hi
            s_cat[128 * b:128 * (b + 1), 384:768] = lo
            s_cat[128 * b:128 * (b + 1), 768:1152] = hi
        tails = jnp.concatenate([full[128:136] * (w[b:b + 1, :] * tri) for b in range(4)], axis=0)
        tails = jnp.concatenate([tails, tails, tails, jnp.zeros_like(tails)], axis=0)
        hi, lo = split(tails)
        s_cat[512:640, 0:384] = hi
        s_cat[512:640, 384:768] = lo
        s_cat[512:640, 768:1152] = hi

        def body(t, _):
            off = pl.multiple_of(t * 128, 128)
            g[s, 0:640, pl.ds(off, 128)] = dot_nt(a_cat[mi], s_cat[pl.ds(off, 128), :])
            return 0

        lax.fori_loop(0, 5, body, 0)
        out(g.at[s], g_out.at[s], 3 + s)

    for s in range(5):
        g[s, 640:672, :] = jnp.zeros((32, 640), F32)
    begin()
    lcopy.wait()
    prep_a(0)
    step1()
    prep_b(0)
    prep_a(1)
    step2()
    prep_b(1)
    prep_a(2)
    step3()
    prep_b(2)
    locals_[0].wait()
    swap.finish()
    synth(0)
    step4()
    synth(1)
    step5()
    synth(2)
    whole(0)
    synth(3)
    whole(1)
    whole(2)
    synth(4)
    step9()
    locals_[1].wait()
    swap.sent()
    for copy in outs:
        copy.wait()
    for n in range(4):
        arrived(f"t{n}", block(columns[n], xh, 1 - core), 0, BLOCK)
        arrived(f"v{n}", block(columns[n], 1 - xh, 1 - core), 0, BLOCK)
    for copy in started:
        copy.wait_send()


def first(spec, own, lat, w, leg):
    hbm = pl.BlockSpec(memory_space=pl.ANY)
    vm = pl.BlockSpec(memory_space=pltpu.VMEM)
    dma = pltpu.SemaphoreType.DMA
    return pl.pallas_call(
        first_kernel,
        out_shape=(jax.ShapeDtypeStruct((16, BLOCK, 128), F32), jax.ShapeDtypeStruct((5, 672, 640), F32),
                   jax.ShapeDtypeStruct((3, 384, 1280), BF)),
        in_specs=[hbm, hbm, vm, vm, hbm],
        out_specs=(hbm, hbm, hbm),
        scratch_shapes=[
            pltpu.VMEM((8, 85, 384), F32),
            pltpu.VMEM((85, 384), F32),
            pltpu.VMEM((3, 384, 640), F32),
            pltpu.VMEM((640, 640), BF),
            pltpu.VMEM((3, 640, 1152), BF),
            pltpu.VMEM((3, 384, 1280), BF),
            pltpu.VMEM((640, 1152), BF),
            pltpu.VMEM((5, 672, 640), F32),
            dma((8,)), dma((8,)), dma((38,)), dma((38,)), dma((3,)), dma((8,)),
        ],
        compiler_params=pltpu.CompilerParams(collective_id=0, has_side_effects=True, vmem_limit_bytes=58 * 2**20),
    )(spec, own, lat, w, leg)


def second_kernel(starts, wt, g_hbm, lp_hbm, cov_hbm, out_ref, cov, lp_cat, g, cv, wcol, gsem, lsem, csem):
    m0, o, first_m = part()
    gcopies = [pltpu.make_async_copy(g_hbm.at[s], g.at[s], gsem.at[s]) for s in range(5)]
    for copy in gcopies:
        copy.start()

    def cov_copy(n):
        return pltpu.make_async_copy(cov_hbm.at[n], cov.at[n], csem.at[n])

    def begin(n, _):
        cov_copy(n).start()
        return 0

    lax.fori_loop(0, 16, begin, 0)
    lcopies = [pltpu.make_async_copy(lp_hbm.at[:, :, pl.ds(src, 640)], lp_cat.at[:, :, pl.ds(dst, 640)], lsem.at[n])
               for n, (src, dst) in enumerate(((0, 0), (0, 640), (640, 1280)))]
    for copy in lcopies:
        copy.start()
    for b in range(4):
        wcol[:, 128 * b:128 * (b + 1)] = jnp.broadcast_to(wt[:, b:b + 1], (384, 128))
    lane = lax.broadcasted_iota(jnp.int32, (384, 128), 1)
    wtail = jnp.zeros((384, 128), F32)
    for b in range(4):
        wtail = jnp.where((lane >= 8 * b) & (lane < 8 * b + 8), wcol[:, 128 * b:128 * (b + 1)], wtail)
    wcol[:, 512:640] = wtail
    for s in range(5):
        cv[s, :, 512:640] = jnp.zeros((672, 128), F32)
    for copy in gcopies:
        copy.wait()

    lane128 = lax.broadcasted_iota(jnp.int32, (1, 128), 1)
    lane32 = lax.broadcasted_iota(jnp.int32, (1, 32), 1)

    def covary(c, _):
        lo_row, hi_row = starts[c], starts[c + 1]
        base = (lo_row // 8) * 8
        blk, odd = c // 2, lax.rem(c, 2)

        @pl.when(odd == 0)
        def _():
            cov_copy(blk).wait()

        top = HALF_BLOCK * odd
        u = cov[blk, 1088:1224, :]
        u = jnp.where(lax.rem(lane128 // 32, 2) == odd, u, pltpu.roll(u, 32, 1))
        u = jnp.concatenate([u[0:128], u[128:136], u[128:136], u[128:136], u[128:136]], axis=0)
        uhi, ulo = split(u)
        ucat = jnp.where(lane128 < 64, uhi.astype(F32), ulo.astype(F32))
        trow = cov[blk, pl.ds(pl.multiple_of(top + 512, 8), 32), :]

        def window(t, _):
            r0 = pl.multiple_of(base + 32 * t, 8)
            x = jnp.concatenate([g[s, pl.ds(r0, 32), :] for s in range(5)], axis=0)
            xhi, xlo = split(x)
            t_hi, t_lo = xhi[:, 512:640].astype(F32), xlo[:, 512:640].astype(F32)
            tcat = jnp.where((lane128 >= 32) & (lane128 < 64), t_lo, t_hi).astype(BF)
            keep = r0 + lax.broadcasted_iota(jnp.int32, (32, 1), 0) >= lo_row
            tail_out = jnp.zeros((160, 32), F32)
            for b in range(4):
                of_b = (lax.rem(lane128, 32) >= 8 * b) & (lax.rem(lane128, 32) < 8 * b + 8)
                ub = jnp.where(of_b, ucat, 0.0).astype(BF)
                main = cov[blk, pl.ds(pl.multiple_of(top + 128 * b, 8), 128), :]
                chi, clo = split(jnp.concatenate([main, trow], axis=0))
                xb = xhi[:, 128 * b:128 * b + 128]
                lhs = jnp.concatenate([xb, xlo[:, 128 * b:128 * b + 128], xb, tcat], axis=1)
                rhs = jnp.concatenate([chi, chi, clo, ub], axis=1)
                res = dot_nt(lhs, rhs)
                for s in range(5):
                    old = cv[s, pl.ds(r0, 32), 128 * b:128 * b + 128]
                    cv[s, pl.ds(r0, 32), 128 * b:128 * b + 128] = jnp.where(keep, res[32 * s:32 * s + 32, 0:128], old)
                tail_out = jnp.where((lane32 >= 8 * b) & (lane32 < 8 * b + 8), res[:, 128:160], tail_out)
            for s in range(5):
                old = cv[s, pl.ds(r0, 32), 512:544]
                cv[s, pl.ds(r0, 32), 512:544] = jnp.where(keep, tail_out[32 * s:32 * s + 32], old)
            return 0

        lax.fori_loop(0, (hi_row - base + 31) // 32, window, 0)
        return 0

    lax.fori_loop(0, 32, covary, 0)
    for copy in lcopies:
        copy.wait()

    for s in range(5):
        mi = (s + o) // 2
        acc = None
        for b in range(5):
            hi, lo = split(cv[s, 0:640, 128 * b:128 * b + 128])
            rhs = jnp.concatenate([hi, lo, hi], axis=0)
            one = jnp.dot(lp_cat[mi], rhs, preferred_element_type=F32)
            one = one * wcol[:, 128 * b:128 * b + 128]
            if b < 4:
                acc = one if acc is None else acc + one
            else:
                tail = one
        tail = tail + pltpu.roll(tail, 128 - 16, 1)
        tail = tail + pltpu.roll(tail, 128 - 8, 1)
        tri = (lax.broadcasted_iota(jnp.int32, (384, 1), 0) >= first_m + mi).astype(F32)
        res = jnp.concatenate([(acc * tri).T, (tail * tri).T[0:8]], axis=0)
        for j in range(8):
            out_ref[j, 17 * s:17 * s + 17, :] = res[17 * j:17 * j + 17]


def second(starts, wt, g, lp, cov):
    hbm = pl.BlockSpec(memory_space=pl.ANY)
    vm = pl.BlockSpec(memory_space=pltpu.VMEM)
    dma = pltpu.SemaphoreType.DMA
    return pl.pallas_call(
        second_kernel,
        out_shape=jax.ShapeDtypeStruct((8, 85, 384), F32),
        in_specs=[pl.BlockSpec(memory_space=pltpu.SMEM), vm, hbm, hbm, hbm],
        out_specs=vm,
        scratch_shapes=[
            pltpu.VMEM((16, BLOCK, 128), F32),
            pltpu.VMEM((3, 384, 1920), BF),
            pltpu.VMEM((5, 672, 640), F32),
            pltpu.VMEM((5, 672, 640), F32),
            pltpu.VMEM((384, 640), F32),
            dma((5,)), dma((3,)), dma((16,)),
        ],
        compiler_params=pltpu.CompilerParams(vmem_limit_bytes=58 * 2**20),
    )(starts, wt, g, lp, cov)


def return_kernel(src, dst, relay, a_send, a_recv, l_sem):
    me = lax.axis_index("lev")
    peers = lev_peers()
    greet(peers)
    met(peers)
    swap = Exchange(src, dst, relay, a_send, a_recv)
    swap.start()
    own = pltpu.make_async_copy(src.at[me], dst.at[me], l_sem)
    own.start()
    swap.hand_on()
    own.wait()
    swap.finish()
    swap.sent()


def give_back(x):
    hbm = pl.BlockSpec(memory_space=pl.ANY)
    dma = pltpu.SemaphoreType.DMA
    return pl.pallas_call(
        return_kernel,
        out_shape=jax.ShapeDtypeStruct(x.shape, F32),
        in_specs=[hbm],
        out_specs=hbm,
        scratch_shapes=[pltpu.VMEM((85, 384), F32), dma((8,)), dma((8,)), dma(())],
        compiler_params=pltpu.CompilerParams(collective_id=1, has_side_effects=True),
    )(x)


def local(spectra, band_filter, band_blocks, legendre, vert_cov, lat_cov):
    w = band_filter * jnp.repeat(band_blocks.astype(F32), 32, axis=1)
    spec = jnp.transpose(spectra, (0, 2, 1, 3)).reshape(8, 85, 384)
    cov, g, lp = first(spec, pack_cov(vert_cov), lat_cov.reshape(1, 640), w, legendre)
    bounds = jnp.arange(40, dtype=jnp.int32)
    starts = jnp.sum((lat_cov[:, None] < bounds[None, :]).astype(jnp.int32), axis=0)
    back = give_back(second(starts, w.T, g, lp, cov)).reshape(20, 2, 17, 384)
    return jnp.transpose(back, (0, 2, 1, 3))


def solution(mesh):
    P = jax.sharding.PartitionSpec
    return jax.shard_map(
        local,
        mesh=mesh,
        in_specs=(P("wave", "lev", None, None), P(), P(), P("wave", None, None), P(None, "wave", None, None), P()),
        out_specs=P("wave", "lev", None, None),
        check_vma=False,
    )
```

```python
import functools
import jax
import jax.numpy as jnp
from jax import lax
from jax.experimental import pallas as pl
from jax.experimental.pallas import tpu as pltpu

F32, BF = jnp.float32, jnp.bfloat16
NT = (((1,), (1,)), ((), ()))
MESH = pl.DeviceIdType.MESH

HALF_BLOCK = 544
BLOCK = 1248
DIRECT = 480
REST = BLOCK - DIRECT
QUARTER = REST // 4


def split(x):
    hi = x.astype(BF)
    return hi, (x - hi.astype(F32)).astype(BF)


def dot_nt(a, b):
    return lax.dot_general(a, b, NT, preferred_element_type=F32)


def pack_cov(vc):
    t = jnp.transpose(vc, (1, 0, 2, 3))
    main = t[:, :, :128, :128].reshape(2, 512, 128)
    rows = t[:, :, 128:, :128].reshape(2, 32, 128)
    u = jnp.transpose(t[:, :, :, 128:], (2, 0, 1, 3)).reshape(136, 64)
    u = jnp.concatenate([u, u], axis=1)
    top = jnp.concatenate([main, rows], axis=1).reshape(2 * HALF_BLOCK, 128)
    return jnp.concatenate([top, u, jnp.zeros((BLOCK - 1224, 128), F32)], axis=0)


def place():
    wave, lev = lax.axis_index("wave"), lax.axis_index("lev")
    return wave // 4, lax.rem(wave // 2, 2), lax.rem(wave, 2), lev // 2, lax.rem(lev, 2)


def at(z, xh, core, y, xl):
    return {"wave": (z * 2 + xh) * 2 + core, "lev": y * 2 + xl}


def lev_peers():
    me = lax.axis_index("lev")
    return [{"lev": lax.rem(me + step, 8)} for step in range(1, 8)]


def greet(peers):
    barrier = pltpu.get_barrier_semaphore()
    for peer in peers:
        pl.semaphore_signal(barrier, inc=1, device_id=peer, device_id_type=MESH)


def met(peers):
    pl.semaphore_wait(pltpu.get_barrier_semaphore(), len(peers))


class Exchange:
    def __init__(self, src, dst, send, recv):
        wave, me = lax.axis_index("wave"), lax.axis_index("lev")
        y, xl = me // 2, lax.rem(me, 2)
        self.copies = []
        for n, (dy, dx) in enumerate(((2, 1), (2, 0), (1, 1), (3, 1), (1, 0), (3, 0), (0, 1))):
            to = lax.rem(y + dy, 4) * 2 + lax.rem(xl + dx, 2)
            self.copies.append(pltpu.make_async_remote_copy(
                src_ref=src.at[to], dst_ref=dst.at[me], send_sem=send.at[n], recv_sem=recv.at[n],
                device_id={"wave": wave, "lev": to}, device_id_type=MESH))

    def start(self):
        for c in self.copies:
            c.start()

    def finish(self):
        for c in self.copies:
            c.wait_recv()

    def sent(self):
        for c in self.copies:
            c.wait_send()


def part():
    lev = lax.axis_index("lev")
    o = lax.rem(lev, 2)
    m0 = 5 * (lev // 2) + 2 * o
    return m0, o, lax.axis_index("wave") * 20 + m0


def first_kernel(spec, own_ref, lat, w, leg, cov_out, g_out, lp_out,
                 s_in, lbuf, perm, a_cat, lp, s_cat, g,
                 a_send, a_recv, c_send, c_recv, l_sem, o_sem):
    z, xh, core, y, xl = place()
    me = lax.axis_index("lev")
    zu, zd, z2 = lax.rem(z + 1, 4), lax.rem(z + 3, 4), lax.rem(z + 2, 4)
    yu, yd, y2 = lax.rem(y + 1, 4), lax.rem(y + 3, 4), lax.rem(y + 2, 4)
    up, down = (at(to, xh, core, y, xl) for to in (zu, zd))
    cross = at(z, 1 - xh, core, y, 1 - xl)
    yup, ydown = (at(z, xh, core, to, xl) for to in (yu, yd))
    twin = at(z, xh, 1 - core, y, xl)
    peers = lev_peers() + [up, down, cross, twin]
    m0, o, first = part()
    greet(peers)
    lcopy = pltpu.make_async_copy(leg.at[pl.ds(m0, 3)], lbuf, l_sem.at[0])
    lcopy.start()

    def block(zz, xx, kk=None):
        return (zz * 2 + xx) * 2 + (core if kk is None else kk)

    own = block(z, xh)
    columns = (z, zd, zu, z2)
    O = [block(c, xh) for c in columns]
    X = [block(c, 1 - xh) for c in columns]
    ids, started = {}, []

    def piece(blk, row, count):
        return cov_out.at[blk, pl.ds(pl.multiple_of(row, 8), count)]

    def send(name, target, blk, row, count, src=None):
        n = ids.setdefault(name, len(ids))
        ref = piece(blk, row, count)
        copy = pltpu.make_async_remote_copy(
            src_ref=ref if src is None else src.at[pl.ds(pl.multiple_of(row, 8), count)], dst_ref=ref,
            send_sem=c_send.at[n], recv_sem=c_recv.at[n], device_id=target, device_id_type=MESH)
        copy.start()
        started.append(copy)

    def arrived(name, blk, row, count):
        n = ids[name]
        ref = piece(blk, row, count)
        pltpu.make_async_remote_copy(
            src_ref=ref, dst_ref=ref, send_sem=c_send.at[n], recv_sem=c_recv.at[n],
            device_id=twin, device_id_type=MESH).wait_recv()

    def quarter(n):
        return DIRECT + QUARTER * n

    swap = Exchange(spec, s_in, a_send, a_recv)

    locals_ = [pltpu.make_async_copy(spec.at[me], s_in.at[me], l_sem.at[1]),
               pltpu.make_async_copy(own_ref, cov_out.at[own], l_sem.at[2])]

    def z_sends(name, blk, row, count, source=None):
        send(name + "u", up, blk, row, count, source)
        send(name + "d", down, blk, row, count, source)

    def z_on(name, blocks, row, count):
        for way, to, blk, first in (("u", up, blocks[1], row), ("d", down, blocks[2], row + count // 2)):
            send(name + "f" + way, to, blk, first, count // 2)

    def z_got(name, blocks, row, count):
        arrived(name + "u", blocks[1], row, count)
        arrived(name + "d", blocks[2], row, count)

    def z_end(name, blocks, row, count):
        arrived(name + "fu", blocks[3], row, count // 2)
        arrived(name + "fd", blocks[3], row + count // 2, count // 2)

    def y_sends(n):
        send(f"yu{n}", yup, X[n], quarter(y), QUARTER)
        send(f"yd{n}", ydown, X[n], quarter(y), QUARTER)

    def y_on(n):
        if n % 2 == 0:
            arrived(f"yu{n}", X[n], quarter(yd), QUARTER)
            send(f"yf{n}", yup, X[n], quarter(yd), QUARTER)
        else:
            arrived(f"yd{n}", X[n], quarter(yu), QUARTER)
            send(f"yf{n}", ydown, X[n], quarter(yu), QUARTER)

    def begin():
        met(peers)
        send("xs", cross, own, quarter(y), QUARTER, own_ref)
        z_sends("D", own, 0, DIRECT, own_ref)
        swap.start()
        send("xD0", cross, own, 0, DIRECT, own_ref)
        for copy in locals_:
            copy.start()

    def step1():
        arrived("xs", X[0], quarter(y), QUARTER)
        z_sends("s", X[0], quarter(y), QUARTER)
        y_sends(0)

    def step2():
        z_got("D", O, 0, DIRECT)
        z_on("D", O, 0, DIRECT)
        send("xD1", cross, O[1], 0, DIRECT)
        send("xD2", cross, O[2], 0, DIRECT)
        z_got("s", X, quarter(y), QUARTER)
        z_on("s", X, quarter(y), QUARTER)
        z_sends("R", own, DIRECT, REST, own_ref)
        send("t0", twin, own, 0, BLOCK, own_ref)
        y_sends(1)
        y_sends(2)

    def step3():
        z_end("D", O, 0, DIRECT)
        send("xD3", cross, O[3], 0, DIRECT)
        z_end("s", X, quarter(y), QUARTER)
        y_sends(3)
        y_on(0)

    def step4():
        y_on(1)
        y_on(2)

    def step5():
        z_got("R", O, DIRECT, REST)
        z_on("R", O, DIRECT, REST)
        send("t1", twin, O[1], 0, BLOCK)
        send("t2", twin, O[2], 0, BLOCK)
        y_on(3)

    def whole(n):
        arrived(f"xD{n}", X[n], 0, DIRECT)
        if n % 2 == 0:
            arrived(f"yd{n}", X[n], quarter(yu), QUARTER)
        else:
            arrived(f"yu{n}", X[n], quarter(yd), QUARTER)
        arrived(f"yf{n}", X[n], quarter(y2), QUARTER)
        send(f"v{n}", twin, X[n], 0, BLOCK)

    def step9():
        z_end("R", O, DIRECT, REST)
        send("t3", twin, O[3], 0, BLOCK)

    outs = []

    def out(src, dst, n):
        copy = pltpu.make_async_copy(src, dst, o_sem.at[n])
        copy.start()
        outs.append(copy)

    def order():
        for s in range(5):
            g[s, 640:672, :] = jnp.zeros((32, 640), F32)
        row = jnp.broadcast_to(lat[...], (8, 640)).astype(F32)
        column = row.T[:, 0:1]
        mine = row[0:1]
        p_row = lax.broadcasted_iota(jnp.int32, (1, 640), 1)
        rank = jnp.zeros((1, 640), F32)
        for t in range(5):
            c = column[128 * t:128 * t + 128]
            p_col = lax.broadcasted_iota(jnp.int32, (128, 1), 0) + 128 * t
            ahead = (c < mine) | ((c == mine) & (p_col < p_row))
            rank = rank + jnp.sum(ahead.astype(F32), axis=0, keepdims=True)
        for t in range(5):
            place_ = (lax.broadcasted_iota(jnp.int32, (128, 640), 0) + 128 * t).astype(F32)
            perm[128 * t:128 * t + 128, :] = (rank == place_).astype(F32).astype(BF)

    def prep_a(mi):
        hi, lo = split(lbuf[mi])
        p = perm[...]
        ahi = dot_nt(p, hi).astype(BF)
        a_cat[mi, :, 0:384] = ahi
        a_cat[mi, :, 384:768] = ahi
        a_cat[mi, :, 768:1152] = dot_nt(p, lo).astype(BF)

    def prep_b(mi):
        hi, lo = split(lbuf[mi])
        p = perm[...]
        lp[mi, :, 0:640] = dot_nt(hi, p).astype(BF)
        lp[mi, :, 640:1280] = dot_nt(lo, p).astype(BF)
        out(lp.at[mi], lp_out.at[mi], mi)

    def synth(s):
        mi = (s + o) // 2
        tri = (lax.broadcasted_iota(jnp.int32, (1, 384), 1) >= first + mi).astype(F32)
        full = jnp.concatenate([s_in[j, 17 * s:17 * s + 17, :] for j in range(8)], axis=0)
        for b in range(4):
            hi, lo = split(full[0:128] * (w[b:b + 1, :] * tri))
            s_cat[128 * b:128 * (b + 1), 0:384] = hi
            s_cat[128 * b:128 * (b + 1), 384:768] = lo
            s_cat[128 * b:128 * (b + 1), 768:1152] = hi
        tails = jnp.concatenate([full[128:136] * (w[b:b + 1, :] * tri) for b in range(4)], axis=0)
        tails = jnp.concatenate([tails, tails, tails, jnp.zeros_like(tails)], axis=0)
        hi, lo = split(tails)
        s_cat[512:640, 0:384] = hi
        s_cat[512:640, 384:768] = lo
        s_cat[512:640, 768:1152] = hi

        def body(t, _):
            off = pl.multiple_of(t * 128, 128)
            g[s, 0:640, pl.ds(off, 128)] = dot_nt(a_cat[mi], s_cat[pl.ds(off, 128), :])
            return 0

        lax.fori_loop(0, 5, body, 0)
        out(g.at[s], g_out.at[s], 3 + s)

    begin()
    order()
    step1()
    lcopy.wait()
    prep_a(0)
    prep_b(0)
    step2()
    prep_a(1)
    prep_b(1)
    step3()
    prep_a(2)
    prep_b(2)
    step4()
    locals_[0].wait()
    swap.finish()
    synth(0)
    step5()
    synth(1)
    synth(2)
    step9()
    synth(3)
    whole(0)
    whole(1)
    synth(4)
    whole(2)
    whole(3)
    locals_[1].wait()
    swap.sent()
    for copy in outs:
        copy.wait()
    for n in range(4):
        arrived(f"t{n}", block(columns[n], xh, 1 - core), 0, BLOCK)
        arrived(f"v{n}", block(columns[n], 1 - xh, 1 - core), 0, BLOCK)
    for copy in started:
        copy.wait_send()


def first(spec, own, lat, w, leg):
    hbm = pl.BlockSpec(memory_space=pl.ANY)
    vm = pl.BlockSpec(memory_space=pltpu.VMEM)
    dma = pltpu.SemaphoreType.DMA
    return pl.pallas_call(
        first_kernel,
        out_shape=(jax.ShapeDtypeStruct((16, BLOCK, 128), F32), jax.ShapeDtypeStruct((5, 672, 640), F32),
                   jax.ShapeDtypeStruct((3, 384, 1280), BF)),
        in_specs=[hbm, vm, vm, vm, hbm],
        out_specs=(hbm, hbm, hbm),
        scratch_shapes=[
            pltpu.VMEM((8, 85, 384), F32),
            pltpu.VMEM((3, 384, 640), F32),
            pltpu.VMEM((640, 640), BF),
            pltpu.VMEM((3, 640, 1152), BF),
            pltpu.VMEM((3, 384, 1280), BF),
            pltpu.VMEM((640, 1152), BF),
            pltpu.VMEM((5, 672, 640), F32),
            dma((7,)), dma((7,)), dma((38,)), dma((38,)), dma((3,)), dma((8,)),
        ],
        compiler_params=pltpu.CompilerParams(collective_id=0, has_side_effects=True, vmem_limit_bytes=58 * 2**20),
    )(spec, own, lat, w, leg)


def second_kernel(starts, wt, g_hbm, lp_hbm, cov_hbm, out_ref, cov, lp_cat, g, cv, wcol, gsem, lsem, csem):
    m0, o, first_m = part()
    gcopies = [pltpu.make_async_copy(g_hbm.at[s], g.at[s], gsem.at[s]) for s in range(5)]
    for copy in gcopies:
        copy.start()

    def cov_copy(n):
        return pltpu.make_async_copy(cov_hbm.at[n], cov.at[n], csem.at[n])

    def begin(n, _):
        cov_copy(n).start()
        return 0

    lax.fori_loop(0, 16, begin, 0)
    lcopies = [pltpu.make_async_copy(lp_hbm.at[:, :, pl.ds(src, 640)], lp_cat.at[:, :, pl.ds(dst, 640)], lsem.at[n])
               for n, (src, dst) in enumerate(((0, 0), (0, 640), (640, 1280)))]
    for copy in lcopies:
        copy.start()
    for b in range(4):
        wcol[:, 128 * b:128 * (b + 1)] = jnp.broadcast_to(wt[:, b:b + 1], (384, 128))
    lane = lax.broadcasted_iota(jnp.int32, (384, 128), 1)
    wtail = jnp.zeros((384, 128), F32)
    for b in range(4):
        wtail = jnp.where((lane >= 8 * b) & (lane < 8 * b + 8), wcol[:, 128 * b:128 * (b + 1)], wtail)
    wcol[:, 512:640] = wtail
    for s in range(5):
        cv[s, :, 512:640] = jnp.zeros((672, 128), F32)
    for copy in gcopies:
        copy.wait()

    lane128 = lax.broadcasted_iota(jnp.int32, (1, 128), 1)
    lane32 = lax.broadcasted_iota(jnp.int32, (1, 32), 1)

    def covary(c, _):
        lo_row, hi_row = starts[c], starts[c + 1]
        base = (lo_row // 8) * 8
        blk, odd = c // 2, lax.rem(c, 2)

        @pl.when(odd == 0)
        def _():
            cov_copy(blk).wait()

        top = HALF_BLOCK * odd
        u = cov[blk, 1088:1224, :]
        u = jnp.where(lax.rem(lane128 // 32, 2) == odd, u, pltpu.roll(u, 32, 1))
        u = jnp.concatenate([u[0:128], u[128:136], u[128:136], u[128:136], u[128:136]], axis=0)
        uhi, ulo = split(u)
        ucat = jnp.where(lane128 < 64, uhi.astype(F32), ulo.astype(F32))
        trow = cov[blk, pl.ds(pl.multiple_of(top + 512, 8), 32), :]

        def window(t, _):
            r0 = pl.multiple_of(base + 32 * t, 8)
            x = jnp.concatenate([g[s, pl.ds(r0, 32), :] for s in range(5)], axis=0)
            xhi, xlo = split(x)
            t_hi, t_lo = xhi[:, 512:640].astype(F32), xlo[:, 512:640].astype(F32)
            tcat = jnp.where((lane128 >= 32) & (lane128 < 64), t_lo, t_hi).astype(BF)
            keep = r0 + lax.broadcasted_iota(jnp.int32, (32, 1), 0) >= lo_row
            tail_out = jnp.zeros((160, 32), F32)
            for b in range(4):
                of_b = (lax.rem(lane128, 32) >= 8 * b) & (lax.rem(lane128, 32) < 8 * b + 8)
                ub = jnp.where(of_b, ucat, 0.0).astype(BF)
                main = cov[blk, pl.ds(pl.multiple_of(top + 128 * b, 8), 128), :]
                chi, clo = split(jnp.concatenate([main, trow], axis=0))
                xb = xhi[:, 128 * b:128 * b + 128]
                lhs = jnp.concatenate([xb, xlo[:, 128 * b:128 * b + 128], xb, tcat], axis=1)
                rhs = jnp.concatenate([chi, chi, clo, ub], axis=1)
                res = dot_nt(lhs, rhs)
                for s in range(5):
                    old = cv[s, pl.ds(r0, 32), 128 * b:128 * b + 128]
                    cv[s, pl.ds(r0, 32), 128 * b:128 * b + 128] = jnp.where(keep, res[32 * s:32 * s + 32, 0:128], old)
                tail_out = jnp.where((lane32 >= 8 * b) & (lane32 < 8 * b + 8), res[:, 128:160], tail_out)
            for s in range(5):
                old = cv[s, pl.ds(r0, 32), 512:544]
                cv[s, pl.ds(r0, 32), 512:544] = jnp.where(keep, tail_out[32 * s:32 * s + 32], old)
            return 0

        lax.fori_loop(0, (hi_row - base + 31) // 32, window, 0)
        return 0

    lax.fori_loop(0, 32, covary, 0)
    for copy in lcopies:
        copy.wait()

    for s in range(5):
        mi = (s + o) // 2
        acc = None
        for b in range(5):
            hi, lo = split(cv[s, 0:640, 128 * b:128 * b + 128])
            rhs = jnp.concatenate([hi, lo, hi], axis=0)
            one = jnp.dot(lp_cat[mi], rhs, preferred_element_type=F32)
            one = one * wcol[:, 128 * b:128 * b + 128]
            if b < 4:
                acc = one if acc is None else acc + one
            else:
                tail = one
        tail = tail + pltpu.roll(tail, 128 - 16, 1)
        tail = tail + pltpu.roll(tail, 128 - 8, 1)
        tri = (lax.broadcasted_iota(jnp.int32, (384, 1), 0) >= first_m + mi).astype(F32)
        res = jnp.concatenate([(acc * tri).T, (tail * tri).T[0:8]], axis=0)
        for j in range(8):
            out_ref[j, 17 * s:17 * s + 17, :] = res[17 * j:17 * j + 17]


def second(starts, wt, g, lp, cov):
    hbm = pl.BlockSpec(memory_space=pl.ANY)
    vm = pl.BlockSpec(memory_space=pltpu.VMEM)
    dma = pltpu.SemaphoreType.DMA
    return pl.pallas_call(
        second_kernel,
        out_shape=jax.ShapeDtypeStruct((8, 85, 384), F32),
        in_specs=[pl.BlockSpec(memory_space=pltpu.SMEM), vm, hbm, hbm, hbm],
        out_specs=vm,
        scratch_shapes=[
            pltpu.VMEM((16, BLOCK, 128), F32),
            pltpu.VMEM((3, 384, 1920), BF),
            pltpu.VMEM((5, 672, 640), F32),
            pltpu.VMEM((5, 672, 640), F32),
            pltpu.VMEM((384, 640), F32),
            dma((5,)), dma((3,)), dma((16,)),
        ],
        compiler_params=pltpu.CompilerParams(vmem_limit_bytes=58 * 2**20),
    )(starts, wt, g, lp, cov)


def return_kernel(src, dst, a_send, a_recv, l_sem):
    me = lax.axis_index("lev")
    peers = lev_peers()
    greet(peers)
    met(peers)
    swap = Exchange(src, dst, a_send, a_recv)
    swap.start()
    own = pltpu.make_async_copy(src.at[me], dst.at[me], l_sem)
    own.start()
    own.wait()
    swap.finish()
    swap.sent()


def give_back(x):
    hbm = pl.BlockSpec(memory_space=pl.ANY)
    vm = pl.BlockSpec(memory_space=pltpu.VMEM)
    dma = pltpu.SemaphoreType.DMA
    return pl.pallas_call(
        return_kernel,
        out_shape=jax.ShapeDtypeStruct(x.shape, F32),
        in_specs=[hbm],
        out_specs=vm,
        scratch_shapes=[dma((7,)), dma((7,)), dma(())],
        compiler_params=pltpu.CompilerParams(collective_id=1, has_side_effects=True),
    )(x)


def local(spectra, band_filter, band_blocks, legendre, vert_cov, lat_cov):
    w = band_filter * jnp.repeat(band_blocks.astype(F32), 32, axis=1)
    spec = jnp.transpose(spectra, (0, 2, 1, 3)).reshape(8, 85, 384)
    cov, g, lp = first(spec, pack_cov(vert_cov), lat_cov.reshape(1, 640), w, legendre)
    bounds = jnp.arange(40, dtype=jnp.int32)
    starts = jnp.sum((lat_cov[:, None] < bounds[None, :]).astype(jnp.int32), axis=0)
    back = give_back(second(starts, w.T, g, lp, cov)).reshape(20, 2, 17, 384)
    return jnp.transpose(back, (0, 2, 1, 3))


def solution(mesh):
    P = jax.sharding.PartitionSpec
    return jax.shard_map(
        local,
        mesh=mesh,
        in_specs=(P("wave", "lev", None, None), P(), P(), P("wave", None, None), P(None, "wave", None, None), P()),
        out_specs=P("wave", "lev", None, None),
        check_vma=False,
    )
```

```python
import functools
import jax
import jax.numpy as jnp
from jax import lax
from jax.experimental import pallas as pl
from jax.experimental.pallas import tpu as pltpu

F32, BF = jnp.float32, jnp.bfloat16
NT = (((1,), (1,)), ((), ()))
MESH = pl.DeviceIdType.MESH

HALF_BLOCK = 544
BLOCK = 1248
DIRECT = 480
REST = BLOCK - DIRECT
QUARTER = REST // 4


def split(x):
    hi = x.astype(BF)
    return hi, (x - hi.astype(F32)).astype(BF)


def dot_nt(a, b):
    return lax.dot_general(a, b, NT, preferred_element_type=F32)


def pack_cov(vc):
    t = jnp.transpose(vc, (1, 0, 2, 3))
    main = t[:, :, :128, :128].reshape(2, 512, 128)
    rows = t[:, :, 128:, :128].reshape(2, 32, 128)
    u = jnp.transpose(t[:, :, :, 128:], (2, 0, 1, 3)).reshape(136, 64)
    u = jnp.concatenate([u, u], axis=1)
    top = jnp.concatenate([main, rows], axis=1).reshape(2 * HALF_BLOCK, 128)
    return jnp.concatenate([top, u, jnp.zeros((BLOCK - 1224, 128), F32)], axis=0)


def place():
    wave, lev = lax.axis_index("wave"), lax.axis_index("lev")
    return wave // 4, lax.rem(wave // 2, 2), lax.rem(wave, 2), lev // 2, lax.rem(lev, 2)


def at(z, xh, core, y, xl):
    return {"wave": (z * 2 + xh) * 2 + core, "lev": y * 2 + xl}


def lev_peers():
    me = lax.axis_index("lev")
    return [{"lev": lax.rem(me + step, 8)} for step in range(1, 8)]


def greet(peers):
    barrier = pltpu.get_barrier_semaphore()
    for peer in peers:
        pl.semaphore_signal(barrier, inc=1, device_id=peer, device_id_type=MESH)


def met(peers):
    pl.semaphore_wait(pltpu.get_barrier_semaphore(), len(peers))


class Exchange:
    def __init__(self, src, dst, send, recv):
        wave, me = lax.axis_index("wave"), lax.axis_index("lev")
        y, xl = me // 2, lax.rem(me, 2)
        self.copies = []
        for n, (dy, dx) in enumerate(((2, 1), (2, 0), (1, 1), (3, 1), (1, 0), (3, 0), (0, 1))):
            to = lax.rem(y + dy, 4) * 2 + lax.rem(xl + dx, 2)
            self.copies.append(pltpu.make_async_remote_copy(
                src_ref=src.at[to], dst_ref=dst.at[me], send_sem=send.at[n], recv_sem=recv.at[n],
                device_id={"wave": wave, "lev": to}, device_id_type=MESH))

    def start(self):
        for c in self.copies:
            c.start()

    def finish(self):
        for c in self.copies:
            c.wait_recv()

    def sent(self):
        for c in self.copies:
            c.wait_send()


def part():
    lev = lax.axis_index("lev")
    o = lax.rem(lev, 2)
    m0 = 5 * (lev // 2) + 2 * o
    return m0, o, lax.axis_index("wave") * 20 + m0


def first_kernel(spec, own_ref, lat, w, leg, cov_out, g_out, lp_out,
                 s_in, lbuf, perm, a_cat, lp, s_cat, g,
                 a_send, a_recv, c_send, c_recv, l_sem, o_sem):
    z, xh, core, y, xl = place()
    me = lax.axis_index("lev")
    zu, zd, z2 = lax.rem(z + 1, 4), lax.rem(z + 3, 4), lax.rem(z + 2, 4)
    yu, yd, y2 = lax.rem(y + 1, 4), lax.rem(y + 3, 4), lax.rem(y + 2, 4)
    up, down = (at(to, xh, core, y, xl) for to in (zu, zd))
    cross = at(z, 1 - xh, core, y, 1 - xl)
    yup, ydown = (at(z, xh, core, to, xl) for to in (yu, yd))
    twin = at(z, xh, 1 - core, y, xl)
    peers = lev_peers() + [up, down, cross, twin]
    m0, o, first = part()
    greet(peers)
    lcopy = pltpu.make_async_copy(leg.at[pl.ds(m0, 3)], lbuf, l_sem.at[0])
    lcopy.start()

    def block(zz, xx, kk=None):
        return (zz * 2 + xx) * 2 + (core if kk is None else kk)

    own = block(z, xh)
    columns = (z, zd, zu, z2)
    O = [block(c, xh) for c in columns]
    X = [block(c, 1 - xh) for c in columns]
    ids, started = {}, []

    def piece(blk, row, count):
        return cov_out.at[blk, pl.ds(pl.multiple_of(row, 8), count)]

    def send(name, target, blk, row, count, src=None):
        n = ids.setdefault(name, len(ids))
        ref = piece(blk, row, count)
        copy = pltpu.make_async_remote_copy(
            src_ref=ref if src is None else src.at[pl.ds(pl.multiple_of(row, 8), count)], dst_ref=ref,
            send_sem=c_send.at[n], recv_sem=c_recv.at[n], device_id=target, device_id_type=MESH)
        copy.start()
        started.append(copy)

    def arrived(name, blk, row, count):
        n = ids[name]
        ref = piece(blk, row, count)
        pltpu.make_async_remote_copy(
            src_ref=ref, dst_ref=ref, send_sem=c_send.at[n], recv_sem=c_recv.at[n],
            device_id=twin, device_id_type=MESH).wait_recv()

    def quarter(n):
        return DIRECT + QUARTER * n

    swap = Exchange(spec, s_in, a_send, a_recv)

    locals_ = [pltpu.make_async_copy(spec.at[me], s_in.at[me], l_sem.at[1]),
               pltpu.make_async_copy(own_ref, cov_out.at[own], l_sem.at[2])]

    def z_sends(name, blk, row, count, source=None):
        send(name + "u", up, blk, row, count, source)
        send(name + "d", down, blk, row, count, source)

    def z_on(name, blocks, row, count):
        for way, to, blk, first in (("u", up, blocks[1], row), ("d", down, blocks[2], row + count // 2)):
            send(name + "f" + way, to, blk, first, count // 2)

    def z_got(name, blocks, row, count):
        arrived(name + "u", blocks[1], row, count)
        arrived(name + "d", blocks[2], row, count)

    def z_end(name, blocks, row, count):
        arrived(name + "fu", blocks[3], row, count // 2)
        arrived(name + "fd", blocks[3], row + count // 2, count // 2)

    def y_sends(n):
        send(f"yu{n}", yup, X[n], quarter(y), QUARTER)
        send(f"yd{n}", ydown, X[n], quarter(y), QUARTER)

    def y_on(n):
        if n % 2 == 0:
            arrived(f"yu{n}", X[n], quarter(yd), QUARTER)
            send(f"yf{n}", yup, X[n], quarter(yd), QUARTER)
        else:
            arrived(f"yd{n}", X[n], quarter(yu), QUARTER)
            send(f"yf{n}", ydown, X[n], quarter(yu), QUARTER)

    def begin():
        met(peers)
        send("xs", cross, own, quarter(y), QUARTER, own_ref)
        z_sends("D", own, 0, DIRECT, own_ref)
        swap.start()
        send("xD0", cross, own, 0, DIRECT, own_ref)
        for copy in locals_:
            copy.start()

    def step1():
        arrived("xs", X[0], quarter(y), QUARTER)
        z_sends("s", X[0], quarter(y), QUARTER)
        y_sends(0)

    def step2():
        z_got("D", O, 0, DIRECT)
        z_on("D", O, 0, DIRECT)
        send("xD1", cross, O[1], 0, DIRECT)
        send("xD2", cross, O[2], 0, DIRECT)
        z_got("s", X, quarter(y), QUARTER)
        z_on("s", X, quarter(y), QUARTER)
        z_sends("R", own, DIRECT, REST, own_ref)
        send("t0", twin, own, 0, BLOCK, own_ref)
        y_sends(1)
        y_sends(2)

    def step3():
        z_end("D", O, 0, DIRECT)
        send("xD3", cross, O[3], 0, DIRECT)
        z_end("s", X, quarter(y), QUARTER)
        y_sends(3)
        y_on(0)

    def step4():
        y_on(1)
        y_on(2)

    def step5():
        z_got("R", O, DIRECT, REST)
        z_on("R", O, DIRECT, REST)
        send("t1", twin, O[1], 0, BLOCK)
        send("t2", twin, O[2], 0, BLOCK)
        y_on(3)

    def whole(n):
        arrived(f"xD{n}", X[n], 0, DIRECT)
        if n % 2 == 0:
            arrived(f"yd{n}", X[n], quarter(yu), QUARTER)
        else:
            arrived(f"yu{n}", X[n], quarter(yd), QUARTER)
        arrived(f"yf{n}", X[n], quarter(y2), QUARTER)
        send(f"v{n}", twin, X[n], 0, BLOCK)

    def step9():
        z_end("R", O, DIRECT, REST)
        send("t3", twin, O[3], 0, BLOCK)

    outs = []

    def out(src, dst, n):
        copy = pltpu.make_async_copy(src, dst, o_sem.at[n])
        copy.start()
        outs.append(copy)

    def order():
        for s in range(5):
            g[s, 640:672, :] = jnp.zeros((32, 640), F32)
        row = jnp.broadcast_to(lat[...], (8, 640)).astype(F32)
        column = row.T[:, 0:1]
        mine = row[0:1]
        p_row = lax.broadcasted_iota(jnp.int32, (1, 640), 1)
        rank = jnp.zeros((1, 640), F32)
        for t in range(5):
            c = column[128 * t:128 * t + 128]
            p_col = lax.broadcasted_iota(jnp.int32, (128, 1), 0) + 128 * t
            ahead = (c < mine) | ((c == mine) & (p_col < p_row))
            rank = rank + jnp.sum(ahead.astype(F32), axis=0, keepdims=True)
        for t in range(5):
            place_ = (lax.broadcasted_iota(jnp.int32, (128, 640), 0) + 128 * t).astype(F32)
            perm[128 * t:128 * t + 128, :] = (rank == place_).astype(F32).astype(BF)

    def prep_a(mi):
        hi, lo = split(lbuf[mi])
        p = perm[...]
        ahi = dot_nt(p, hi).astype(BF)
        a_cat[mi, :, 0:384] = ahi
        a_cat[mi, :, 384:768] = ahi
        a_cat[mi, :, 768:1152] = dot_nt(p, lo).astype(BF)

    def prep_b(mi):
        hi, lo = split(lbuf[mi])
        p = perm[...]
        lp[mi, :, 0:640] = dot_nt(hi, p).astype(BF)
        lp[mi, :, 640:1280] = dot_nt(lo, p).astype(BF)
        out(lp.at[mi], lp_out.at[mi], mi)

    def synth(s):
        mi = (s + o) // 2
        tri = (lax.broadcasted_iota(jnp.int32, (1, 384), 1) >= first + mi).astype(F32)
        full = jnp.concatenate([s_in[j, 17 * s:17 * s + 17, :] for j in range(8)], axis=0)
        for b in range(4):
            hi, lo = split(full[0:128] * (w[b:b + 1, :] * tri))
            s_cat[128 * b:128 * (b + 1), 0:384] = hi
            s_cat[128 * b:128 * (b + 1), 384:768] = lo
            s_cat[128 * b:128 * (b + 1), 768:1152] = hi
        tails = jnp.concatenate([full[128:136] * (w[b:b + 1, :] * tri) for b in range(4)], axis=0)
        tails = jnp.concatenate([tails, tails, tails, jnp.zeros_like(tails)], axis=0)
        hi, lo = split(tails)
        s_cat[512:640, 0:384] = hi
        s_cat[512:640, 384:768] = lo
        s_cat[512:640, 768:1152] = hi

        def body(t, _):
            off = pl.multiple_of(t * 256, 256)
            g[s, 0:640, pl.ds(off, 256)] = dot_nt(a_cat[mi], s_cat[pl.ds(off, 256), :])
            return 0

        lax.fori_loop(0, 2, body, 0)
        g[s, 0:640, 512:640] = dot_nt(a_cat[mi], s_cat[512:640, :])
        out(g.at[s], g_out.at[s], 3 + s)

    begin()
    order()
    step1()
    lcopy.wait()
    prep_a(0)
    prep_b(0)
    step2()
    prep_a(1)
    prep_b(1)
    step3()
    prep_a(2)
    prep_b(2)
    step4()
    locals_[0].wait()
    swap.finish()
    synth(0)
    step5()
    synth(1)
    synth(2)
    step9()
    synth(3)
    whole(0)
    whole(1)
    synth(4)
    whole(2)
    whole(3)
    locals_[1].wait()
    swap.sent()
    for copy in outs:
        copy.wait()
    for n in range(4):
        arrived(f"t{n}", block(columns[n], xh, 1 - core), 0, BLOCK)
        arrived(f"v{n}", block(columns[n], 1 - xh, 1 - core), 0, BLOCK)
    for copy in started:
        copy.wait_send()


def first(spec, own, lat, w, leg):
    hbm = pl.BlockSpec(memory_space=pl.ANY)
    vm = pl.BlockSpec(memory_space=pltpu.VMEM)
    dma = pltpu.SemaphoreType.DMA
    return pl.pallas_call(
        first_kernel,
        out_shape=(jax.ShapeDtypeStruct((16, BLOCK, 128), F32), jax.ShapeDtypeStruct((5, 672, 640), F32),
                   jax.ShapeDtypeStruct((3, 384, 1280), BF)),
        in_specs=[hbm, vm, vm, vm, hbm],
        out_specs=(hbm, hbm, hbm),
        scratch_shapes=[
            pltpu.VMEM((8, 85, 384), F32),
            pltpu.VMEM((3, 384, 640), F32),
            pltpu.VMEM((640, 640), BF),
            pltpu.VMEM((3, 640, 1152), BF),
            pltpu.VMEM((3, 384, 1280), BF),
            pltpu.VMEM((640, 1152), BF),
            pltpu.VMEM((5, 672, 640), F32),
            dma((7,)), dma((7,)), dma((38,)), dma((38,)), dma((3,)), dma((8,)),
        ],
        compiler_params=pltpu.CompilerParams(collective_id=0, has_side_effects=True, vmem_limit_bytes=58 * 2**20),
    )(spec, own, lat, w, leg)


def second_kernel(starts, wt, g_hbm, lp_hbm, cov_hbm, out_ref, cov, lp_cat, g, cv, wcol, gsem, lsem, csem):
    m0, o, first_m = part()
    gcopies = [pltpu.make_async_copy(g_hbm.at[s], g.at[s], gsem.at[s]) for s in range(5)]
    for copy in gcopies:
        copy.start()

    def cov_copy(n):
        return pltpu.make_async_copy(cov_hbm.at[n], cov.at[n], csem.at[n])

    def begin(n, _):
        cov_copy(n).start()
        return 0

    lax.fori_loop(0, 16, begin, 0)
    lcopies = [pltpu.make_async_copy(lp_hbm.at[:, :, pl.ds(src, 640)], lp_cat.at[:, :, pl.ds(dst, 640)], lsem.at[n])
               for n, (src, dst) in enumerate(((0, 0), (0, 640), (640, 1280)))]
    for copy in lcopies:
        copy.start()
    for b in range(4):
        wcol[:, 128 * b:128 * (b + 1)] = jnp.broadcast_to(wt[:, b:b + 1], (384, 128))
    lane = lax.broadcasted_iota(jnp.int32, (384, 128), 1)
    wtail = jnp.zeros((384, 128), F32)
    for b in range(4):
        wtail = jnp.where((lane >= 8 * b) & (lane < 8 * b + 8), wcol[:, 128 * b:128 * (b + 1)], wtail)
    wcol[:, 512:640] = wtail
    for s in range(5):
        cv[s, :, 512:640] = jnp.zeros((672, 128), F32)
    for copy in gcopies:
        copy.wait()

    lane128 = lax.broadcasted_iota(jnp.int32, (1, 128), 1)
    lane32 = lax.broadcasted_iota(jnp.int32, (1, 32), 1)

    def side(c, blk, odd):
        u = cov[blk, 1088:1224, :]
        u = jnp.where(lax.rem(lane128 // 32, 2) == odd, u, pltpu.roll(u, 32, 1))
        u = jnp.concatenate([u[0:128], u[128:136], u[128:136], u[128:136], u[128:136]], axis=0)
        uhi, ulo = split(u)
        return jnp.where(lane128 < 64, uhi.astype(F32), ulo.astype(F32))

    def window(c, blk, odd, ucat, r0, lo_row, hi_row):
        top = HALF_BLOCK * odd
        trow = cov[blk, top + 512:top + 544, :]
        x = jnp.concatenate([g[s, pl.ds(r0, 32), :] for s in range(5)], axis=0)
        xhi, xlo = split(x)
        t_hi, t_lo = xhi[:, 512:640].astype(F32), xlo[:, 512:640].astype(F32)
        tcat = jnp.where((lane128 >= 32) & (lane128 < 64), t_lo, t_hi).astype(BF)
        row = r0 + lax.broadcasted_iota(jnp.int32, (32, 1), 0)
        keep = (row >= lo_row) & (row < hi_row)
        tail_out = jnp.zeros((160, 32), F32)
        made = []
        for b in range(4):
            of_b = (lax.rem(lane128, 32) >= 8 * b) & (lax.rem(lane128, 32) < 8 * b + 8)
            ub = jnp.where(of_b, ucat, 0.0).astype(BF)
            chi, clo = split(jnp.concatenate([cov[blk, top + 128 * b:top + 128 * b + 128, :], trow], axis=0))
            xb = xhi[:, 128 * b:128 * b + 128]
            lhs = jnp.concatenate([xb, xlo[:, 128 * b:128 * b + 128], xb, tcat], axis=1)
            rhs = jnp.concatenate([chi, chi, clo, ub], axis=1)
            res = dot_nt(lhs, rhs)
            made.append(res[:, 0:128])
            tail_out = jnp.where((lane32 >= 8 * b) & (lane32 < 8 * b + 8), res[:, 128:160], tail_out)
        return r0, keep, made, tail_out

    def put(r0, keep, made, tail_out):
        for s in range(5):
            for b in range(4):
                old = cv[s, pl.ds(r0, 32), 128 * b:128 * b + 128]
                cv[s, pl.ds(r0, 32), 128 * b:128 * b + 128] = jnp.where(keep, made[b][32 * s:32 * s + 32], old)
            old = cv[s, pl.ds(r0, 32), 512:544]
            cv[s, pl.ds(r0, 32), 512:544] = jnp.where(keep, tail_out[32 * s:32 * s + 32], old)

    def covary(blk, _):
        cov_copy(blk).wait()
        firsts = []
        for odd in range(2):
            c = 2 * blk + odd
            lo_row, hi_row = starts[c], starts[c + 1]
            base = jnp.minimum((lo_row // 8) * 8, 632)
            ucat = side(c, blk, odd)
            firsts.append(window(c, blk, odd, ucat, pl.multiple_of(base, 8), lo_row, hi_row))
        for one in firsts:
            put(*one)
        for odd in range(2):
            c = 2 * blk + odd
            lo_row, hi_row = starts[c], starts[c + 1]
            base = jnp.minimum((lo_row // 8) * 8, 632)

            def more(t, _):
                put(*window(c, blk, odd, side(c, blk, odd), pl.multiple_of(base + 32 * t, 8), lo_row, hi_row))
                return 0

            lax.fori_loop(1, (hi_row - base + 31) // 32, more, 0)
        return 0

    lax.fori_loop(0, 16, covary, 0)
    for copy in lcopies:
        copy.wait()

    for s in range(5):
        mi = (s + o) // 2
        acc = None
        for b, wide in ((0, 256), (256, 256), (512, 128)):
            hi, lo = split(cv[s, 0:640, b:b + wide])
            rhs = jnp.concatenate([hi, lo, hi], axis=0)
            one = jnp.dot(lp_cat[mi], rhs, preferred_element_type=F32)
            one = one * wcol[:, b:b + wide]
            if b < 512:
                one = one[:, 0:128] + one[:, 128:256]
                acc = one if acc is None else acc + one
            else:
                tail = one
        tail = tail + pltpu.roll(tail, 128 - 16, 1)
        tail = tail + pltpu.roll(tail, 128 - 8, 1)
        tri = (lax.broadcasted_iota(jnp.int32, (384, 1), 0) >= first_m + mi).astype(F32)
        res = jnp.concatenate([(acc * tri).T, (tail * tri).T[0:8]], axis=0)
        for j in range(8):
            out_ref[j, 17 * s:17 * s + 17, :] = res[17 * j:17 * j + 17]


def second(starts, wt, g, lp, cov):
    hbm = pl.BlockSpec(memory_space=pl.ANY)
    vm = pl.BlockSpec(memory_space=pltpu.VMEM)
    dma = pltpu.SemaphoreType.DMA
    return pl.pallas_call(
        second_kernel,
        out_shape=jax.ShapeDtypeStruct((8, 85, 384), F32),
        in_specs=[pl.BlockSpec(memory_space=pltpu.SMEM), vm, hbm, hbm, hbm],
        out_specs=vm,
        scratch_shapes=[
            pltpu.VMEM((16, BLOCK, 128), F32),
            pltpu.VMEM((3, 384, 1920), BF),
            pltpu.VMEM((5, 672, 640), F32),
            pltpu.VMEM((5, 672, 640), F32),
            pltpu.VMEM((384, 640), F32),
            dma((5,)), dma((3,)), dma((16,)),
        ],
        compiler_params=pltpu.CompilerParams(vmem_limit_bytes=58 * 2**20),
    )(starts, wt, g, lp, cov)


def return_kernel(src, dst, a_send, a_recv, l_sem):
    me = lax.axis_index("lev")
    peers = lev_peers()
    greet(peers)
    met(peers)
    swap = Exchange(src, dst, a_send, a_recv)
    swap.start()
    own = pltpu.make_async_copy(src.at[me], dst.at[me], l_sem)
    own.start()
    own.wait()
    swap.finish()
    swap.sent()


def give_back(x):
    hbm = pl.BlockSpec(memory_space=pl.ANY)
    vm = pl.BlockSpec(memory_space=pltpu.VMEM)
    dma = pltpu.SemaphoreType.DMA
    return pl.pallas_call(
        return_kernel,
        out_shape=jax.ShapeDtypeStruct(x.shape, F32),
        in_specs=[hbm],
        out_specs=vm,
        scratch_shapes=[dma((7,)), dma((7,)), dma(())],
        compiler_params=pltpu.CompilerParams(collective_id=1, has_side_effects=True),
    )(x)


def local(spectra, band_filter, band_blocks, legendre, vert_cov, lat_cov):
    w = band_filter * jnp.repeat(band_blocks.astype(F32), 32, axis=1)
    spec = jnp.transpose(spectra, (0, 2, 1, 3)).reshape(8, 85, 384)
    cov, g, lp = first(spec, pack_cov(vert_cov), lat_cov.reshape(1, 640), w, legendre)
    bounds = jnp.arange(40, dtype=jnp.int32)
    starts = jnp.sum((lat_cov[:, None] < bounds[None, :]).astype(jnp.int32), axis=0)
    back = give_back(second(starts, w.T, g, lp, cov)).reshape(20, 2, 17, 384)
    return jnp.transpose(back, (0, 2, 1, 3))


def solution(mesh):
    P = jax.sharding.PartitionSpec
    return jax.shard_map(
        local,
        mesh=mesh,
        in_specs=(P("wave", "lev", None, None), P(), P(), P("wave", None, None), P(None, "wave", None, None), P()),
        out_specs=P("wave", "lev", None, None),
        check_vma=False,
    )
```

```python
import functools
import jax
import jax.numpy as jnp
from jax import lax
from jax.experimental import pallas as pl
from jax.experimental.pallas import tpu as pltpu

F32, BF = jnp.float32, jnp.bfloat16
NT = (((1,), (1,)), ((), ()))
MESH = pl.DeviceIdType.MESH

HALF_BLOCK = 544
BLOCK = 1248
DIRECT = 480
REST = BLOCK - DIRECT
QUARTER = REST // 4


def split(x):
    hi = x.astype(BF)
    return hi, (x - hi.astype(F32)).astype(BF)


def dot_nt(a, b):
    return lax.dot_general(a, b, NT, preferred_element_type=F32)


def pack_cov(vc, side, own):
    side[...] = jnp.zeros((136, 128), F32)
    u = jnp.zeros((136, 128), F32)
    for c in range(2):
        for b in range(4):
            own[HALF_BLOCK * c + 128 * b:HALF_BLOCK * c + 128 * b + 128, :] = vc[b, c, 0:128, 0:128]
            own[HALF_BLOCK * c + 512 + 8 * b:HALF_BLOCK * c + 520 + 8 * b, :] = vc[b, c, 128:136, 0:128]
            side[:, 0:8] = vc[b, c, :, 128:136]
            at_lane = 32 * c + 8 * b
            u = u + (pltpu.roll(side[...], at_lane, 1) if at_lane else side[...])
    own[1088:1224, :] = u + pltpu.roll(u, 64, 1)
    own[1224:BLOCK, :] = jnp.zeros((BLOCK - 1224, 128), F32)


def place():
    wave, lev = lax.axis_index("wave"), lax.axis_index("lev")
    return wave // 4, lax.rem(wave // 2, 2), lax.rem(wave, 2), lev // 2, lax.rem(lev, 2)


def at(z, xh, core, y, xl):
    return {"wave": (z * 2 + xh) * 2 + core, "lev": y * 2 + xl}


def lev_peers():
    me = lax.axis_index("lev")
    return [{"lev": lax.rem(me + step, 8)} for step in range(1, 8)]


def greet(peers):
    barrier = pltpu.get_barrier_semaphore()
    for peer in peers:
        pl.semaphore_signal(barrier, inc=1, device_id=peer, device_id_type=MESH)


def met(peers):
    pl.semaphore_wait(pltpu.get_barrier_semaphore(), len(peers))


class Exchange:
    def __init__(self, src, dst, send, recv):
        wave, me = lax.axis_index("wave"), lax.axis_index("lev")
        y, xl = me // 2, lax.rem(me, 2)
        self.copies = []
        for n, (dy, dx) in enumerate(((2, 1), (2, 0), (1, 1), (3, 1), (1, 0), (3, 0), (0, 1))):
            to = lax.rem(y + dy, 4) * 2 + lax.rem(xl + dx, 2)
            self.copies.append(pltpu.make_async_remote_copy(
                src_ref=src.at[to], dst_ref=dst.at[me], send_sem=send.at[n], recv_sem=recv.at[n],
                device_id={"wave": wave, "lev": to}, device_id_type=MESH))

    def start(self):
        for c in self.copies:
            c.start()

    def finish(self):
        for c in self.copies:
            c.wait_recv()

    def sent(self):
        for c in self.copies:
            c.wait_send()


def part():
    lev = lax.axis_index("lev")
    o = lax.rem(lev, 2)
    m0 = 5 * (lev // 2) + 2 * o
    return m0, o, lax.axis_index("wave") * 20 + m0


def first_kernel(spec, vc, lat, band_filter, band_blocks, leg, cov_out, g_out, lp_out,
                 own_ref, side, w, s_in, lbuf, perm, a_cat, lp, s_cat, g,
                 a_send, a_recv, c_send, c_recv, l_sem, o_sem):
    z, xh, core, y, xl = place()
    me = lax.axis_index("lev")
    zu, zd, z2 = lax.rem(z + 1, 4), lax.rem(z + 3, 4), lax.rem(z + 2, 4)
    yu, yd, y2 = lax.rem(y + 1, 4), lax.rem(y + 3, 4), lax.rem(y + 2, 4)
    up, down = (at(to, xh, core, y, xl) for to in (zu, zd))
    cross = at(z, 1 - xh, core, y, 1 - xl)
    yup, ydown = (at(z, xh, core, to, xl) for to in (yu, yd))
    twin = at(z, xh, 1 - core, y, xl)
    peers = lev_peers() + [up, down, cross, twin]
    m0, o, first = part()
    greet(peers)
    lcopy = pltpu.make_async_copy(leg.at[pl.ds(m0, 3)], lbuf, l_sem.at[0])
    lcopy.start()
    pack_cov(vc, side, own_ref)
    keep = jnp.zeros((4, 384), F32)
    block_of = lax.broadcasted_iota(jnp.int32, (4, 384), 1) // 32
    for n in range(12):
        keep = jnp.where(block_of == n, band_blocks[:, n:n + 1].astype(F32), keep)
    w[...] = band_filter[...] * keep

    def block(zz, xx, kk=None):
        return (zz * 2 + xx) * 2 + (core if kk is None else kk)

    own = block(z, xh)
    columns = (z, zd, zu, z2)
    O = [block(c, xh) for c in columns]
    X = [block(c, 1 - xh) for c in columns]
    ids, started = {}, []

    def piece(blk, row, count):
        return cov_out.at[blk, pl.ds(pl.multiple_of(row, 8), count)]

    def send(name, target, blk, row, count, src=None):
        n = ids.setdefault(name, len(ids))
        ref = piece(blk, row, count)
        copy = pltpu.make_async_remote_copy(
            src_ref=ref if src is None else src.at[pl.ds(pl.multiple_of(row, 8), count)], dst_ref=ref,
            send_sem=c_send.at[n], recv_sem=c_recv.at[n], device_id=target, device_id_type=MESH)
        copy.start()
        started.append(copy)

    def arrived(name, blk, row, count):
        n = ids[name]
        ref = piece(blk, row, count)
        pltpu.make_async_remote_copy(
            src_ref=ref, dst_ref=ref, send_sem=c_send.at[n], recv_sem=c_recv.at[n],
            device_id=twin, device_id_type=MESH).wait_recv()

    def quarter(n):
        return DIRECT + QUARTER * n

    swap = Exchange(spec, s_in, a_send, a_recv)

    locals_ = [pltpu.make_async_copy(spec.at[me], s_in.at[me], l_sem.at[1]),
               pltpu.make_async_copy(own_ref, cov_out.at[own], l_sem.at[2])]

    def z_sends(name, blk, row, count, source=None):
        send(name + "u", up, blk, row, count, source)
        send(name + "d", down, blk, row, count, source)

    def z_on(name, blocks, row, count):
        for way, to, blk, first in (("u", up, blocks[1], row), ("d", down, blocks[2], row + count // 2)):
            send(name + "f" + way, to, blk, first, count // 2)

    def z_got(name, blocks, row, count):
        arrived(name + "u", blocks[1], row, count)
        arrived(name + "d", blocks[2], row, count)

    def z_end(name, blocks, row, count):
        arrived(name + "fu", blocks[3], row, count // 2)
        arrived(name + "fd", blocks[3], row + count // 2, count // 2)

    def y_sends(n):
        send(f"yu{n}", yup, X[n], quarter(y), QUARTER)
        send(f"yd{n}", ydown, X[n], quarter(y), QUARTER)

    def y_on(n):
        if n % 2 == 0:
            arrived(f"yu{n}", X[n], quarter(yd), QUARTER)
            send(f"yf{n}", yup, X[n], quarter(yd), QUARTER)
        else:
            arrived(f"yd{n}", X[n], quarter(yu), QUARTER)
            send(f"yf{n}", ydown, X[n], quarter(yu), QUARTER)

    def begin():
        met(peers)
        send("xs", cross, own, quarter(y), QUARTER, own_ref)
        z_sends("D", own, 0, DIRECT, own_ref)
        swap.start()
        send("xD0", cross, own, 0, DIRECT, own_ref)
        for copy in locals_:
            copy.start()

    def step1():
        arrived("xs", X[0], quarter(y), QUARTER)
        z_sends("s", X[0], quarter(y), QUARTER)
        y_sends(0)

    def step2():
        z_got("D", O, 0, DIRECT)
        z_on("D", O, 0, DIRECT)
        send("xD1", cross, O[1], 0, DIRECT)
        send("xD2", cross, O[2], 0, DIRECT)
        z_got("s", X, quarter(y), QUARTER)
        z_on("s", X, quarter(y), QUARTER)
        z_sends("R", own, DIRECT, REST, own_ref)
        send("t0", twin, own, 0, BLOCK, own_ref)
        y_sends(1)
        y_sends(2)

    def step3():
        z_end("D", O, 0, DIRECT)
        send("xD3", cross, O[3], 0, DIRECT)
        z_end("s", X, quarter(y), QUARTER)
        y_sends(3)
        y_on(0)

    def step4():
        y_on(1)
        y_on(2)

    def step5():
        z_got("R", O, DIRECT, REST)
        z_on("R", O, DIRECT, REST)
        send("t1", twin, O[1], 0, BLOCK)
        send("t2", twin, O[2], 0, BLOCK)
        y_on(3)

    def whole(n):
        arrived(f"xD{n}", X[n], 0, DIRECT)
        if n % 2 == 0:
            arrived(f"yd{n}", X[n], quarter(yu), QUARTER)
        else:
            arrived(f"yu{n}", X[n], quarter(yd), QUARTER)
        arrived(f"yf{n}", X[n], quarter(y2), QUARTER)
        send(f"v{n}", twin, X[n], 0, BLOCK)

    def step9():
        z_end("R", O, DIRECT, REST)
        send("t3", twin, O[3], 0, BLOCK)

    outs = []

    def out(src, dst, n):
        copy = pltpu.make_async_copy(src, dst, o_sem.at[n])
        copy.start()
        outs.append(copy)

    def order():
        for s in range(5):
            g[s, 640:672, :] = jnp.zeros((32, 640), F32)
        row = jnp.broadcast_to(lat[...].reshape(1, 640), (8, 640)).astype(F32)
        column = row.T[:, 0:1]
        mine = row[0:1]
        p_row = lax.broadcasted_iota(jnp.int32, (1, 640), 1)
        rank = jnp.zeros((1, 640), F32)
        for t in range(5):
            c = column[128 * t:128 * t + 128]
            p_col = lax.broadcasted_iota(jnp.int32, (128, 1), 0) + 128 * t
            ahead = (c < mine) | ((c == mine) & (p_col < p_row))
            rank = rank + jnp.sum(ahead.astype(F32), axis=0, keepdims=True)
        for t in range(5):
            place_ = (lax.broadcasted_iota(jnp.int32, (128, 640), 0) + 128 * t).astype(F32)
            perm[128 * t:128 * t + 128, :] = (rank == place_).astype(F32).astype(BF)

    def prep_a(mi):
        hi, lo = split(lbuf[mi])
        p = perm[...]
        ahi = dot_nt(p, hi).astype(BF)
        a_cat[mi, :, 0:384] = ahi
        a_cat[mi, :, 384:768] = ahi
        a_cat[mi, :, 768:1152] = dot_nt(p, lo).astype(BF)

    def prep_b(mi):
        hi, lo = split(lbuf[mi])
        p = perm[...]
        lp[mi, :, 0:640] = dot_nt(hi, p).astype(BF)
        lp[mi, :, 640:1280] = dot_nt(lo, p).astype(BF)
        out(lp.at[mi], lp_out.at[mi], mi)

    def synth(s):
        mi = (s + o) // 2
        tri = (lax.broadcasted_iota(jnp.int32, (1, 384), 1) >= first + mi).astype(F32)
        full = jnp.concatenate([s_in[j, 17 * s:17 * s + 17, :] for j in range(8)], axis=0)
        for b in range(4):
            hi, lo = split(full[0:128] * (w[b:b + 1, :] * tri))
            s_cat[128 * b:128 * (b + 1), 0:384] = hi
            s_cat[128 * b:128 * (b + 1), 384:768] = lo
            s_cat[128 * b:128 * (b + 1), 768:1152] = hi
        tails = jnp.concatenate([full[128:136] * (w[b:b + 1, :] * tri) for b in range(4)], axis=0)
        tails = jnp.concatenate([tails, tails, tails, jnp.zeros_like(tails)], axis=0)
        hi, lo = split(tails)
        s_cat[512:640, 0:384] = hi
        s_cat[512:640, 384:768] = lo
        s_cat[512:640, 768:1152] = hi

        def body(t, _):
            off = pl.multiple_of(t * 256, 256)
            g[s, 0:640, pl.ds(off, 256)] = dot_nt(a_cat[mi], s_cat[pl.ds(off, 256), :])
            return 0

        lax.fori_loop(0, 2, body, 0)
        g[s, 0:640, 512:640] = dot_nt(a_cat[mi], s_cat[512:640, :])
        out(g.at[s], g_out.at[s], 3 + s)

    begin()
    order()
    step1()
    lcopy.wait()
    prep_a(0)
    prep_b(0)
    step2()
    prep_a(1)
    prep_b(1)
    step3()
    prep_a(2)
    prep_b(2)
    step4()
    locals_[0].wait()
    swap.finish()
    synth(0)
    step5()
    synth(1)
    synth(2)
    step9()
    synth(3)
    whole(0)
    whole(1)
    synth(4)
    whole(2)
    whole(3)
    locals_[1].wait()
    swap.sent()
    for copy in outs:
        copy.wait()
    for n in range(4):
        arrived(f"t{n}", block(columns[n], xh, 1 - core), 0, BLOCK)
        arrived(f"v{n}", block(columns[n], 1 - xh, 1 - core), 0, BLOCK)
    for copy in started:
        copy.wait_send()


def first(spec, vc, lat, band_filter, band_blocks, leg):
    hbm = pl.BlockSpec(memory_space=pl.ANY)
    vm = pl.BlockSpec(memory_space=pltpu.VMEM)
    dma = pltpu.SemaphoreType.DMA
    return pl.pallas_call(
        first_kernel,
        out_shape=(jax.ShapeDtypeStruct((16, BLOCK, 128), F32), jax.ShapeDtypeStruct((5, 672, 640), F32),
                   jax.ShapeDtypeStruct((3, 384, 1280), BF)),
        in_specs=[hbm, vm, vm, vm, vm, hbm],
        out_specs=(hbm, hbm, hbm),
        scratch_shapes=[
            pltpu.VMEM((BLOCK, 128), F32),
            pltpu.VMEM((136, 128), F32),
            pltpu.VMEM((4, 384), F32),
            pltpu.VMEM((8, 85, 384), F32),
            pltpu.VMEM((3, 384, 640), F32),
            pltpu.VMEM((640, 640), BF),
            pltpu.VMEM((3, 640, 1152), BF),
            pltpu.VMEM((3, 384, 1280), BF),
            pltpu.VMEM((640, 1152), BF),
            pltpu.VMEM((5, 672, 640), F32),
            dma((7,)), dma((7,)), dma((38,)), dma((38,)), dma((3,)), dma((8,)),
        ],
        compiler_params=pltpu.CompilerParams(collective_id=0, has_side_effects=True, vmem_limit_bytes=58 * 2**20),
    )(spec, vc, lat, band_filter, band_blocks, leg)


def second_kernel(starts, wt, g_hbm, lp_hbm, cov_hbm, out_ref, cov, lp_cat, g, cv, wcol, gsem, lsem, csem):
    m0, o, first_m = part()
    gcopies = [pltpu.make_async_copy(g_hbm.at[s], g.at[s], gsem.at[s]) for s in range(5)]
    for copy in gcopies:
        copy.start()

    def cov_copy(n):
        return pltpu.make_async_copy(cov_hbm.at[n], cov.at[n], csem.at[n])

    def begin(n, _):
        cov_copy(n).start()
        return 0

    lax.fori_loop(0, 16, begin, 0)
    lcopies = [pltpu.make_async_copy(lp_hbm.at[:, :, pl.ds(src, 640)], lp_cat.at[:, :, pl.ds(dst, 640)], lsem.at[n])
               for n, (src, dst) in enumerate(((0, 0), (0, 640), (640, 1280)))]
    for copy in lcopies:
        copy.start()
    for b in range(4):
        wcol[:, 128 * b:128 * (b + 1)] = jnp.broadcast_to(wt[:, b:b + 1], (384, 128))
    lane = lax.broadcasted_iota(jnp.int32, (384, 128), 1)
    wtail = jnp.zeros((384, 128), F32)
    for b in range(4):
        wtail = jnp.where((lane >= 8 * b) & (lane < 8 * b + 8), wcol[:, 128 * b:128 * (b + 1)], wtail)
    wcol[:, 512:640] = wtail
    for s in range(5):
        cv[s, :, 512:640] = jnp.zeros((672, 128), F32)
    for copy in gcopies:
        copy.wait()

    lane128 = lax.broadcasted_iota(jnp.int32, (1, 128), 1)
    lane32 = lax.broadcasted_iota(jnp.int32, (1, 32), 1)

    def side(c, blk, odd):
        u = cov[blk, 1088:1224, :]
        u = jnp.where(lax.rem(lane128 // 32, 2) == odd, u, pltpu.roll(u, 32, 1))
        u = jnp.concatenate([u[0:128], u[128:136], u[128:136], u[128:136], u[128:136]], axis=0)
        uhi, ulo = split(u)
        return jnp.where(lane128 < 64, uhi.astype(F32), ulo.astype(F32))

    def window(c, blk, odd, ucat, r0, lo_row, hi_row):
        top = HALF_BLOCK * odd
        trow = cov[blk, top + 512:top + 544, :]
        x = jnp.concatenate([g[s, pl.ds(r0, 32), :] for s in range(5)], axis=0)
        xhi, xlo = split(x)
        t_hi, t_lo = xhi[:, 512:640].astype(F32), xlo[:, 512:640].astype(F32)
        tcat = jnp.where((lane128 >= 32) & (lane128 < 64), t_lo, t_hi).astype(BF)
        row = r0 + lax.broadcasted_iota(jnp.int32, (32, 1), 0)
        keep = (row >= lo_row) & (row < hi_row)
        tail_out = jnp.zeros((160, 32), F32)
        made = []
        for b in range(4):
            of_b = (lax.rem(lane128, 32) >= 8 * b) & (lax.rem(lane128, 32) < 8 * b + 8)
            ub = jnp.where(of_b, ucat, 0.0).astype(BF)
            chi, clo = split(jnp.concatenate([cov[blk, top + 128 * b:top + 128 * b + 128, :], trow], axis=0))
            xb = xhi[:, 128 * b:128 * b + 128]
            lhs = jnp.concatenate([xb, xlo[:, 128 * b:128 * b + 128], xb, tcat], axis=1)
            rhs = jnp.concatenate([chi, chi, clo, ub], axis=1)
            res = dot_nt(lhs, rhs)
            made.append(res[:, 0:128])
            tail_out = jnp.where((lane32 >= 8 * b) & (lane32 < 8 * b + 8), res[:, 128:160], tail_out)
        return r0, keep, made, tail_out

    def put(r0, keep, made, tail_out):
        for s in range(5):
            for b in range(4):
                old = cv[s, pl.ds(r0, 32), 128 * b:128 * b + 128]
                cv[s, pl.ds(r0, 32), 128 * b:128 * b + 128] = jnp.where(keep, made[b][32 * s:32 * s + 32], old)
            old = cv[s, pl.ds(r0, 32), 512:544]
            cv[s, pl.ds(r0, 32), 512:544] = jnp.where(keep, tail_out[32 * s:32 * s + 32], old)

    def covary(blk, _):
        cov_copy(blk).wait()
        firsts = []
        for odd in range(2):
            c = 2 * blk + odd
            lo_row, hi_row = starts[c], starts[c + 1]
            base = jnp.minimum((lo_row // 8) * 8, 632)
            ucat = side(c, blk, odd)
            firsts.append(window(c, blk, odd, ucat, pl.multiple_of(base, 8), lo_row, hi_row))
        for one in firsts:
            put(*one)
        for odd in range(2):
            c = 2 * blk + odd
            lo_row, hi_row = starts[c], starts[c + 1]
            base = jnp.minimum((lo_row // 8) * 8, 632)

            def more(t, _):
                put(*window(c, blk, odd, side(c, blk, odd), pl.multiple_of(base + 32 * t, 8), lo_row, hi_row))
                return 0

            lax.fori_loop(1, (hi_row - base + 31) // 32, more, 0)
        return 0

    lax.fori_loop(0, 16, covary, 0)
    for copy in lcopies:
        copy.wait()

    for s in range(5):
        mi = (s + o) // 2
        acc = None
        for b, wide in ((0, 256), (256, 256), (512, 128)):
            hi, lo = split(cv[s, 0:640, b:b + wide])
            rhs = jnp.concatenate([hi, lo, hi], axis=0)
            one = jnp.dot(lp_cat[mi], rhs, preferred_element_type=F32)
            one = one * wcol[:, b:b + wide]
            if b < 512:
                one = one[:, 0:128] + one[:, 128:256]
                acc = one if acc is None else acc + one
            else:
                tail = one
        tail = tail + pltpu.roll(tail, 128 - 16, 1)
        tail = tail + pltpu.roll(tail, 128 - 8, 1)
        tri = (lax.broadcasted_iota(jnp.int32, (384, 1), 0) >= first_m + mi).astype(F32)
        res = jnp.concatenate([(acc * tri).T, (tail * tri).T[0:8]], axis=0)
        for j in range(8):
            out_ref[j, 17 * s:17 * s + 17, :] = res[17 * j:17 * j + 17]


def second(starts, wt, g, lp, cov):
    hbm = pl.BlockSpec(memory_space=pl.ANY)
    vm = pl.BlockSpec(memory_space=pltpu.VMEM)
    dma = pltpu.SemaphoreType.DMA
    return pl.pallas_call(
        second_kernel,
        out_shape=jax.ShapeDtypeStruct((8, 85, 384), F32),
        in_specs=[pl.BlockSpec(memory_space=pltpu.SMEM), vm, hbm, hbm, hbm],
        out_specs=vm,
        scratch_shapes=[
            pltpu.VMEM((16, BLOCK, 128), F32),
            pltpu.VMEM((3, 384, 1920), BF),
            pltpu.VMEM((5, 672, 640), F32),
            pltpu.VMEM((5, 672, 640), F32),
            pltpu.VMEM((384, 640), F32),
            dma((5,)), dma((3,)), dma((16,)),
        ],
        compiler_params=pltpu.CompilerParams(vmem_limit_bytes=58 * 2**20),
    )(starts, wt, g, lp, cov)


def return_kernel(src, out, dst, a_send, a_recv, l_sem):
    me = lax.axis_index("lev")
    peers = lev_peers()
    greet(peers)
    met(peers)
    swap = Exchange(src, dst, a_send, a_recv)
    swap.start()
    own = pltpu.make_async_copy(src.at[me], dst.at[me], l_sem)
    own.start()
    own.wait()
    swap.finish()
    for j in range(8):
        for s in range(5):
            out[5 * j + s] = dst[j, 17 * s:17 * s + 17, :]
    swap.sent()


def give_back(x):
    hbm = pl.BlockSpec(memory_space=pl.ANY)
    vm = pl.BlockSpec(memory_space=pltpu.VMEM)
    dma = pltpu.SemaphoreType.DMA
    return pl.pallas_call(
        return_kernel,
        out_shape=jax.ShapeDtypeStruct((40, 17, 384), F32),
        in_specs=[hbm],
        out_specs=vm,
        scratch_shapes=[pltpu.VMEM(x.shape, F32), dma((7,)), dma((7,)), dma(())],
        compiler_params=pltpu.CompilerParams(collective_id=1, has_side_effects=True),
    )(x)


def local(spectra, band_filter, band_blocks, legendre, vert_cov, lat_cov):
    w = band_filter * jnp.repeat(band_blocks.astype(F32), 32, axis=1)
    spec = jnp.transpose(spectra, (0, 2, 1, 3)).reshape(8, 85, 384)
    cov, g, lp = first(spec, vert_cov, lat_cov, band_filter, band_blocks, legendre)
    bounds = jnp.arange(40, dtype=jnp.int32)
    starts = jnp.sum((lat_cov[:, None] < bounds[None, :]).astype(jnp.int32), axis=0)
    back = give_back(second(starts, w.T, g, lp, cov)).reshape(20, 2, 17, 384)
    return jnp.transpose(back, (0, 2, 1, 3))


def solution(mesh):
    P = jax.sharding.PartitionSpec
    return jax.shard_map(
        local,
        mesh=mesh,
        in_specs=(P("wave", "lev", None, None), P(), P(), P("wave", None, None), P(None, "wave", None, None), P()),
        out_specs=P("wave", "lev", None, None),
        check_vma=False,
    )
```

```python
import functools
import jax
import jax.numpy as jnp
from jax import lax
from jax.experimental import pallas as pl
from jax.experimental.pallas import tpu as pltpu

F32, BF = jnp.float32, jnp.bfloat16
NT = (((1,), (1,)), ((), ()))
MESH = pl.DeviceIdType.MESH

HALF_BLOCK = 544
BLOCK = 1248
DIRECT = 480
REST = BLOCK - DIRECT
QUARTER = REST // 4


def split(x):
    hi = x.astype(BF)
    return hi, (x - hi.astype(F32)).astype(BF)


def dot_nt(a, b):
    return lax.dot_general(a, b, NT, preferred_element_type=F32)


def pack_cov(vc, side, own):
    side[...] = jnp.zeros((136, 128), F32)
    u = jnp.zeros((136, 128), F32)
    for c in range(2):
        for b in range(4):
            own[HALF_BLOCK * c + 128 * b:HALF_BLOCK * c + 128 * b + 128, :] = vc[b, c, 0:128, 0:128]
            own[HALF_BLOCK * c + 512 + 8 * b:HALF_BLOCK * c + 520 + 8 * b, :] = vc[b, c, 128:136, 0:128]
            side[:, 0:8] = vc[b, c, :, 128:136]
            at_lane = 32 * c + 8 * b
            u = u + (pltpu.roll(side[...], at_lane, 1) if at_lane else side[...])
    own[1088:1224, :] = u + pltpu.roll(u, 64, 1)
    own[1224:BLOCK, :] = jnp.zeros((BLOCK - 1224, 128), F32)


def place():
    wave, lev = lax.axis_index("wave"), lax.axis_index("lev")
    return wave // 4, lax.rem(wave // 2, 2), lax.rem(wave, 2), lev // 2, lax.rem(lev, 2)


def at(z, xh, core, y, xl):
    return {"wave": (z * 2 + xh) * 2 + core, "lev": y * 2 + xl}


def lev_peers():
    me = lax.axis_index("lev")
    return [{"lev": lax.rem(me + step, 8)} for step in range(1, 8)]


def greet(peers):
    barrier = pltpu.get_barrier_semaphore()
    for peer in peers:
        pl.semaphore_signal(barrier, inc=1, device_id=peer, device_id_type=MESH)


def met(peers):
    pl.semaphore_wait(pltpu.get_barrier_semaphore(), len(peers))


class Exchange:
    def __init__(self, src, dst, send, recv):
        wave, me = lax.axis_index("wave"), lax.axis_index("lev")
        y, xl = me // 2, lax.rem(me, 2)
        self.copies = []
        for n, (dy, dx) in enumerate(((2, 1), (2, 0), (1, 1), (3, 1), (1, 0), (3, 0), (0, 1))):
            to = lax.rem(y + dy, 4) * 2 + lax.rem(xl + dx, 2)
            self.copies.append(pltpu.make_async_remote_copy(
                src_ref=src.at[to], dst_ref=dst.at[me], send_sem=send.at[n], recv_sem=recv.at[n],
                device_id={"wave": wave, "lev": to}, device_id_type=MESH))

    def start(self):
        for c in self.copies:
            c.start()

    def finish(self):
        for c in self.copies:
            c.wait_recv()

    def sent(self):
        for c in self.copies:
            c.wait_send()


def part():
    lev = lax.axis_index("lev")
    o = lax.rem(lev, 2)
    m0 = 5 * (lev // 2) + 2 * o
    return m0, o, lax.axis_index("wave") * 20 + m0


def band_weights(band_filter, band_blocks):
    keep = jnp.zeros((4, 384), F32)
    block_of = lax.broadcasted_iota(jnp.int32, (4, 384), 1) // 32
    for n in range(12):
        keep = jnp.where(block_of == n, band_blocks[:, n:n + 1].astype(F32), keep)
    return band_filter[...] * keep


def first_kernel(spec, vc, lat, band_filter, band_blocks, leg, cov_out, g_out, lp_out,
                 own_ref, side, w, s_in, lbuf, perm, a_cat, lp, s_cat, g,
                 a_send, a_recv, c_send, c_recv, l_sem, o_sem):
    z, xh, core, y, xl = place()
    me = lax.axis_index("lev")
    zu, zd, z2 = lax.rem(z + 1, 4), lax.rem(z + 3, 4), lax.rem(z + 2, 4)
    yu, yd, y2 = lax.rem(y + 1, 4), lax.rem(y + 3, 4), lax.rem(y + 2, 4)
    up, down = (at(to, xh, core, y, xl) for to in (zu, zd))
    cross = at(z, 1 - xh, core, y, 1 - xl)
    yup, ydown = (at(z, xh, core, to, xl) for to in (yu, yd))
    twin = at(z, xh, 1 - core, y, xl)
    peers = lev_peers() + [up, down, cross, twin]
    m0, o, first = part()
    greet(peers)
    lcopy = pltpu.make_async_copy(leg.at[pl.ds(m0, 3)], lbuf, l_sem.at[0])
    lcopy.start()
    pack_cov(vc, side, own_ref)
    w[...] = band_weights(band_filter, band_blocks)

    def block(zz, xx, kk=None):
        return (zz * 2 + xx) * 2 + (core if kk is None else kk)

    own = block(z, xh)
    columns = (z, zd, zu, z2)
    O = [block(c, xh) for c in columns]
    X = [block(c, 1 - xh) for c in columns]
    ids, started = {}, []

    def piece(blk, row, count):
        return cov_out.at[blk, pl.ds(pl.multiple_of(row, 8), count)]

    def send(name, target, blk, row, count, src=None):
        n = ids.setdefault(name, len(ids))
        ref = piece(blk, row, count)
        copy = pltpu.make_async_remote_copy(
            src_ref=ref if src is None else src.at[pl.ds(pl.multiple_of(row, 8), count)], dst_ref=ref,
            send_sem=c_send.at[n], recv_sem=c_recv.at[n], device_id=target, device_id_type=MESH)
        copy.start()
        started.append(copy)

    def arrived(name, blk, row, count):
        n = ids[name]
        ref = piece(blk, row, count)
        pltpu.make_async_remote_copy(
            src_ref=ref, dst_ref=ref, send_sem=c_send.at[n], recv_sem=c_recv.at[n],
            device_id=twin, device_id_type=MESH).wait_recv()

    def quarter(n):
        return DIRECT + QUARTER * n

    swap = Exchange(spec, s_in, a_send, a_recv)

    locals_ = [pltpu.make_async_copy(spec.at[me], s_in.at[me], l_sem.at[1]),
               pltpu.make_async_copy(own_ref, cov_out.at[own], l_sem.at[2])]

    def z_sends(name, blk, row, count, source=None):
        send(name + "u", up, blk, row, count, source)
        send(name + "d", down, blk, row, count, source)

    def z_on(name, blocks, row, count):
        for way, to, blk, first in (("u", up, blocks[1], row), ("d", down, blocks[2], row + count // 2)):
            send(name + "f" + way, to, blk, first, count // 2)

    def z_got(name, blocks, row, count):
        arrived(name + "u", blocks[1], row, count)
        arrived(name + "d", blocks[2], row, count)

    def z_end(name, blocks, row, count):
        arrived(name + "fu", blocks[3], row, count // 2)
        arrived(name + "fd", blocks[3], row + count // 2, count // 2)

    def y_sends(n):
        send(f"yu{n}", yup, X[n], quarter(y), QUARTER)
        send(f"yd{n}", ydown, X[n], quarter(y), QUARTER)

    def y_on(n):
        if n % 2 == 0:
            arrived(f"yu{n}", X[n], quarter(yd), QUARTER)
            send(f"yf{n}", yup, X[n], quarter(yd), QUARTER)
        else:
            arrived(f"yd{n}", X[n], quarter(yu), QUARTER)
            send(f"yf{n}", ydown, X[n], quarter(yu), QUARTER)

    def begin():
        met(peers)
        send("xs", cross, own, quarter(y), QUARTER, own_ref)
        z_sends("D", own, 0, DIRECT, own_ref)
        swap.start()
        send("xD0", cross, own, 0, DIRECT, own_ref)
        for copy in locals_:
            copy.start()

    def step1():
        arrived("xs", X[0], quarter(y), QUARTER)
        z_sends("s", X[0], quarter(y), QUARTER)
        y_sends(0)

    def step2():
        z_got("D", O, 0, DIRECT)
        z_on("D", O, 0, DIRECT)
        send("xD1", cross, O[1], 0, DIRECT)
        send("xD2", cross, O[2], 0, DIRECT)
        z_got("s", X, quarter(y), QUARTER)
        z_on("s", X, quarter(y), QUARTER)
        z_sends("R", own, DIRECT, REST, own_ref)
        send("t0", twin, own, 0, BLOCK, own_ref)
        y_sends(1)
        y_sends(2)

    def step3():
        z_end("D", O, 0, DIRECT)
        send("xD3", cross, O[3], 0, DIRECT)
        z_end("s", X, quarter(y), QUARTER)
        y_sends(3)
        y_on(0)

    def step4():
        y_on(1)
        y_on(2)

    def step5():
        z_got("R", O, DIRECT, REST)
        z_on("R", O, DIRECT, REST)
        send("t1", twin, O[1], 0, BLOCK)
        send("t2", twin, O[2], 0, BLOCK)
        y_on(3)

    def whole(n):
        arrived(f"xD{n}", X[n], 0, DIRECT)
        if n % 2 == 0:
            arrived(f"yd{n}", X[n], quarter(yu), QUARTER)
        else:
            arrived(f"yu{n}", X[n], quarter(yd), QUARTER)
        arrived(f"yf{n}", X[n], quarter(y2), QUARTER)
        send(f"v{n}", twin, X[n], 0, BLOCK)

    def step9():
        z_end("R", O, DIRECT, REST)
        send("t3", twin, O[3], 0, BLOCK)

    outs = []

    def out(src, dst, n):
        copy = pltpu.make_async_copy(src, dst, o_sem.at[n])
        copy.start()
        outs.append(copy)

    def order():
        for s in range(5):
            g[s, 640:672, :] = jnp.zeros((32, 640), F32)
        row = jnp.broadcast_to(lat[...].reshape(1, 640), (8, 640)).astype(F32)
        column = row.T[:, 0:1]
        mine = row[0:1]
        p_row = lax.broadcasted_iota(jnp.int32, (1, 640), 1)
        rank = jnp.zeros((1, 640), F32)
        for t in range(5):
            c = column[128 * t:128 * t + 128]
            p_col = lax.broadcasted_iota(jnp.int32, (128, 1), 0) + 128 * t
            ahead = (c < mine) | ((c == mine) & (p_col < p_row))
            rank = rank + jnp.sum(ahead.astype(F32), axis=0, keepdims=True)
        for t in range(5):
            place_ = (lax.broadcasted_iota(jnp.int32, (128, 640), 0) + 128 * t).astype(F32)
            perm[128 * t:128 * t + 128, :] = (rank == place_).astype(F32).astype(BF)

    def prep_a(mi):
        hi, lo = split(lbuf[mi])
        p = perm[...]
        ahi = dot_nt(p, hi).astype(BF)
        a_cat[mi, :, 0:384] = ahi
        a_cat[mi, :, 384:768] = ahi
        a_cat[mi, :, 768:1152] = dot_nt(p, lo).astype(BF)

    def prep_b(mi):
        hi, lo = split(lbuf[mi])
        p = perm[...]
        lp[mi, :, 0:640] = dot_nt(hi, p).astype(BF)
        lp[mi, :, 640:1280] = dot_nt(lo, p).astype(BF)
        out(lp.at[mi], lp_out.at[mi], mi)

    def synth(s):
        mi = (s + o) // 2
        tri = (lax.broadcasted_iota(jnp.int32, (1, 384), 1) >= first + mi).astype(F32)
        full = jnp.concatenate([s_in[j, 17 * s:17 * s + 17, :] for j in range(8)], axis=0)
        for b in range(4):
            hi, lo = split(full[0:128] * (w[b:b + 1, :] * tri))
            s_cat[128 * b:128 * (b + 1), 0:384] = hi
            s_cat[128 * b:128 * (b + 1), 384:768] = lo
            s_cat[128 * b:128 * (b + 1), 768:1152] = hi
        tails = jnp.concatenate([full[128:136] * (w[b:b + 1, :] * tri) for b in range(4)], axis=0)
        tails = jnp.concatenate([tails, tails, tails, jnp.zeros_like(tails)], axis=0)
        hi, lo = split(tails)
        s_cat[512:640, 0:384] = hi
        s_cat[512:640, 384:768] = lo
        s_cat[512:640, 768:1152] = hi

        def body(t, _):
            off = pl.multiple_of(t * 256, 256)
            g[s, 0:640, pl.ds(off, 256)] = dot_nt(a_cat[mi], s_cat[pl.ds(off, 256), :])
            return 0

        lax.fori_loop(0, 2, body, 0)
        g[s, 0:640, 512:640] = dot_nt(a_cat[mi], s_cat[512:640, :])
        out(g.at[s], g_out.at[s], 3 + s)

    begin()
    order()
    step1()
    lcopy.wait()
    prep_a(0)
    prep_a(1)
    step2()
    prep_a(2)
    prep_b(0)
    step3()
    prep_b(1)
    prep_b(2)
    step4()
    locals_[0].wait()
    swap.finish()
    synth(0)
    step5()
    synth(1)
    synth(2)
    synth(3)
    step9()
    whole(0)
    whole(1)
    synth(4)
    whole(2)
    whole(3)
    locals_[1].wait()
    swap.sent()
    for copy in outs:
        copy.wait()
    for n in range(4):
        arrived(f"t{n}", block(columns[n], xh, 1 - core), 0, BLOCK)
        arrived(f"v{n}", block(columns[n], 1 - xh, 1 - core), 0, BLOCK)
    for copy in started:
        copy.wait_send()


def first(spec, vc, lat, band_filter, band_blocks, leg):
    hbm = pl.BlockSpec(memory_space=pl.ANY)
    vm = pl.BlockSpec(memory_space=pltpu.VMEM)
    dma = pltpu.SemaphoreType.DMA
    return pl.pallas_call(
        first_kernel,
        out_shape=(jax.ShapeDtypeStruct((16, BLOCK, 128), F32), jax.ShapeDtypeStruct((5, 672, 640), F32),
                   jax.ShapeDtypeStruct((3, 384, 1280), BF)),
        in_specs=[hbm, vm, vm, vm, vm, hbm],
        out_specs=(hbm, hbm, hbm),
        scratch_shapes=[
            pltpu.VMEM((BLOCK, 128), F32),
            pltpu.VMEM((136, 128), F32),
            pltpu.VMEM((4, 384), F32),
            pltpu.VMEM((8, 85, 384), F32),
            pltpu.VMEM((3, 384, 640), F32),
            pltpu.VMEM((640, 640), BF),
            pltpu.VMEM((3, 640, 1152), BF),
            pltpu.VMEM((3, 384, 1280), BF),
            pltpu.VMEM((640, 1152), BF),
            pltpu.VMEM((5, 672, 640), F32),
            dma((7,)), dma((7,)), dma((38,)), dma((38,)), dma((3,)), dma((8,)),
        ],
        compiler_params=pltpu.CompilerParams(collective_id=0, has_side_effects=True, vmem_limit_bytes=58 * 2**20),
    )(spec, vc, lat, band_filter, band_blocks, leg)


def second_kernel(starts, band_filter, band_blocks, g_hbm, lp_hbm, cov_hbm, out_ref, cov, lp_cat, g, cv, wcol, gsem, lsem, csem):
    m0, o, first_m = part()
    gcopies = [pltpu.make_async_copy(g_hbm.at[s], g.at[s], gsem.at[s]) for s in range(5)]
    for copy in gcopies:
        copy.start()

    def cov_copy(n):
        return pltpu.make_async_copy(cov_hbm.at[n], cov.at[n], csem.at[n])

    def begin(n, _):
        cov_copy(n).start()
        return 0

    lax.fori_loop(0, 16, begin, 0)
    lcopies = [pltpu.make_async_copy(lp_hbm.at[:, :, pl.ds(src, 640)], lp_cat.at[:, :, pl.ds(dst, 640)], lsem.at[n])
               for n, (src, dst) in enumerate(((0, 0), (0, 640), (640, 1280)))]
    for copy in lcopies:
        copy.start()
    w = band_weights(band_filter, band_blocks)
    wt = jnp.concatenate([w, w], axis=0).T
    for b in range(4):
        wcol[:, 128 * b:128 * (b + 1)] = jnp.broadcast_to(wt[:, b:b + 1], (384, 128))
    lane = lax.broadcasted_iota(jnp.int32, (384, 128), 1)
    wtail = jnp.zeros((384, 128), F32)
    for b in range(4):
        wtail = jnp.where((lane >= 8 * b) & (lane < 8 * b + 8), wcol[:, 128 * b:128 * (b + 1)], wtail)
    wcol[:, 512:640] = wtail
    for s in range(5):
        cv[s, :, 512:640] = jnp.zeros((672, 128), F32)
    for copy in gcopies:
        copy.wait()

    lane128 = lax.broadcasted_iota(jnp.int32, (1, 128), 1)
    lane32 = lax.broadcasted_iota(jnp.int32, (1, 32), 1)

    def side(c, blk, odd):
        u = cov[blk, 1088:1224, :]
        u = jnp.where(lax.rem(lane128 // 32, 2) == odd, u, pltpu.roll(u, 32, 1))
        u = jnp.concatenate([u[0:128], u[128:136], u[128:136], u[128:136], u[128:136]], axis=0)
        uhi, ulo = split(u)
        return jnp.where(lane128 < 64, uhi.astype(F32), ulo.astype(F32))

    def window(c, blk, odd, ucat, r0, lo_row, hi_row):
        top = HALF_BLOCK * odd
        trow = cov[blk, top + 512:top + 544, :]
        x = jnp.concatenate([g[s, pl.ds(r0, 32), :] for s in range(5)], axis=0)
        xhi, xlo = split(x)
        t_hi, t_lo = xhi[:, 512:640].astype(F32), xlo[:, 512:640].astype(F32)
        tcat = jnp.where((lane128 >= 32) & (lane128 < 64), t_lo, t_hi).astype(BF)
        row = r0 + lax.broadcasted_iota(jnp.int32, (32, 1), 0)
        keep = (row >= lo_row) & (row < hi_row)
        tail_out = jnp.zeros((160, 32), F32)
        made = []
        for b in range(4):
            of_b = (lax.rem(lane128, 32) >= 8 * b) & (lax.rem(lane128, 32) < 8 * b + 8)
            ub = jnp.where(of_b, ucat, 0.0).astype(BF)
            chi, clo = split(jnp.concatenate([cov[blk, top + 128 * b:top + 128 * b + 128, :], trow], axis=0))
            xb = xhi[:, 128 * b:128 * b + 128]
            lhs = jnp.concatenate([xb, xlo[:, 128 * b:128 * b + 128], xb, tcat], axis=1)
            rhs = jnp.concatenate([chi, chi, clo, ub], axis=1)
            res = dot_nt(lhs, rhs)
            made.append(res[:, 0:128])
            tail_out = jnp.where((lane32 >= 8 * b) & (lane32 < 8 * b + 8), res[:, 128:160], tail_out)
        return r0, keep, made, tail_out

    def put(r0, keep, made, tail_out):
        for s in range(5):
            for b in range(4):
                old = cv[s, pl.ds(r0, 32), 128 * b:128 * b + 128]
                cv[s, pl.ds(r0, 32), 128 * b:128 * b + 128] = jnp.where(keep, made[b][32 * s:32 * s + 32], old)
            old = cv[s, pl.ds(r0, 32), 512:544]
            cv[s, pl.ds(r0, 32), 512:544] = jnp.where(keep, tail_out[32 * s:32 * s + 32], old)

    def covary(blk, _):
        cov_copy(blk).wait()
        firsts = []
        for odd in range(2):
            c = 2 * blk + odd
            lo_row, hi_row = starts[c], starts[c + 1]
            base = jnp.minimum((lo_row // 8) * 8, 632)
            ucat = side(c, blk, odd)
            firsts.append(window(c, blk, odd, ucat, pl.multiple_of(base, 8), lo_row, hi_row))
        for one in firsts:
            put(*one)
        for odd in range(2):
            c = 2 * blk + odd
            lo_row, hi_row = starts[c], starts[c + 1]
            base = jnp.minimum((lo_row // 8) * 8, 632)

            def more(t, _):
                put(*window(c, blk, odd, side(c, blk, odd), pl.multiple_of(base + 32 * t, 8), lo_row, hi_row))
                return 0

            lax.fori_loop(1, (hi_row - base + 31) // 32, more, 0)
        return 0

    lax.fori_loop(0, 16, covary, 0)
    for copy in lcopies:
        copy.wait()

    for s in range(5):
        mi = (s + o) // 2
        acc = None
        for b, wide in ((0, 256), (256, 256), (512, 128)):
            hi, lo = split(cv[s, 0:640, b:b + wide])
            rhs = jnp.concatenate([hi, lo, hi], axis=0)
            one = jnp.dot(lp_cat[mi], rhs, preferred_element_type=F32)
            one = one * wcol[:, b:b + wide]
            if b < 512:
                one = one[:, 0:128] + one[:, 128:256]
                acc = one if acc is None else acc + one
            else:
                tail = one
        tail = tail + pltpu.roll(tail, 128 - 16, 1)
        tail = tail + pltpu.roll(tail, 128 - 8, 1)
        tri = (lax.broadcasted_iota(jnp.int32, (384, 1), 0) >= first_m + mi).astype(F32)
        res = jnp.concatenate([(acc * tri).T, (tail * tri).T[0:8]], axis=0)
        for j in range(8):
            out_ref[j, 17 * s:17 * s + 17, :] = res[17 * j:17 * j + 17]


def second(starts, band_filter, band_blocks, g, lp, cov):
    hbm = pl.BlockSpec(memory_space=pl.ANY)
    vm = pl.BlockSpec(memory_space=pltpu.VMEM)
    dma = pltpu.SemaphoreType.DMA
    return pl.pallas_call(
        second_kernel,
        out_shape=jax.ShapeDtypeStruct((8, 85, 384), F32),
        in_specs=[pl.BlockSpec(memory_space=pltpu.SMEM), vm, vm, hbm, hbm, hbm],
        out_specs=vm,
        scratch_shapes=[
            pltpu.VMEM((16, BLOCK, 128), F32),
            pltpu.VMEM((3, 384, 1920), BF),
            pltpu.VMEM((5, 672, 640), F32),
            pltpu.VMEM((5, 672, 640), F32),
            pltpu.VMEM((384, 640), F32),
            dma((5,)), dma((3,)), dma((16,)),
        ],
        compiler_params=pltpu.CompilerParams(vmem_limit_bytes=58 * 2**20),
    )(starts, band_filter, band_blocks, g, lp, cov)


def return_kernel(src, out, dst, a_send, a_recv, l_sem):
    me = lax.axis_index("lev")
    peers = lev_peers()
    greet(peers)
    met(peers)
    swap = Exchange(src, dst, a_send, a_recv)
    swap.start()
    own = pltpu.make_async_copy(src.at[me], dst.at[me], l_sem)
    own.start()
    own.wait()
    swap.finish()
    for j in range(8):
        for s in range(5):
            out[5 * j + s] = dst[j, 17 * s:17 * s + 17, :]
    swap.sent()


def give_back(x):
    hbm = pl.BlockSpec(memory_space=pl.ANY)
    vm = pl.BlockSpec(memory_space=pltpu.VMEM)
    dma = pltpu.SemaphoreType.DMA
    return pl.pallas_call(
        return_kernel,
        out_shape=jax.ShapeDtypeStruct((40, 17, 384), F32),
        in_specs=[hbm],
        out_specs=vm,
        scratch_shapes=[pltpu.VMEM(x.shape, F32), dma((7,)), dma((7,)), dma(())],
        compiler_params=pltpu.CompilerParams(collective_id=1, has_side_effects=True),
    )(x)


def local(spectra, band_filter, band_blocks, legendre, vert_cov, lat_cov):
    spec = jnp.transpose(spectra, (0, 2, 1, 3)).reshape(8, 85, 384)
    cov, g, lp = first(spec, vert_cov, lat_cov, band_filter, band_blocks, legendre)
    bounds = jnp.arange(40, dtype=jnp.int32)
    starts = jnp.sum((lat_cov[:, None] < bounds[None, :]).astype(jnp.int32), axis=0)
    back = give_back(second(starts, band_filter, band_blocks, g, lp, cov)).reshape(20, 2, 17, 384)
    return jnp.transpose(back, (0, 2, 1, 3))


def solution(mesh):
    P = jax.sharding.PartitionSpec
    return jax.shard_map(
        local,
        mesh=mesh,
        in_specs=(P("wave", "lev", None, None), P(), P(), P("wave", None, None), P(None, "wave", None, None), P()),
        out_specs=P("wave", "lev", None, None),
        check_vma=False,
    )
```

```python
import functools
import jax
import jax.numpy as jnp
from jax import lax
from jax.experimental import pallas as pl
from jax.experimental.pallas import tpu as pltpu

F32, BF = jnp.float32, jnp.bfloat16
NT = (((1,), (1,)), ((), ()))
MESH = pl.DeviceIdType.MESH

HALF_BLOCK = 544
BLOCK = 1248
DIRECT = 480
REST = BLOCK - DIRECT
QUARTER = REST // 4


def split(x):
    hi = x.astype(BF)
    return hi, (x - hi.astype(F32)).astype(BF)


def dot_nt(a, b):
    return lax.dot_general(a, b, NT, preferred_element_type=F32)


def pack_cov(vc, side, own):
    side[...] = jnp.zeros((136, 128), F32)
    u = jnp.zeros((136, 128), F32)
    for c in range(2):
        for b in range(4):
            own[HALF_BLOCK * c + 128 * b:HALF_BLOCK * c + 128 * b + 128, :] = vc[b, c, 0:128, 0:128]
            own[HALF_BLOCK * c + 512 + 8 * b:HALF_BLOCK * c + 520 + 8 * b, :] = vc[b, c, 128:136, 0:128]
            side[:, 0:8] = vc[b, c, :, 128:136]
            at_lane = 32 * c + 8 * b
            u = u + (pltpu.roll(side[...], at_lane, 1) if at_lane else side[...])
    own[1088:1224, :] = u + pltpu.roll(u, 64, 1)
    own[1224:BLOCK, :] = jnp.zeros((BLOCK - 1224, 128), F32)


def place():
    wave, lev = lax.axis_index("wave"), lax.axis_index("lev")
    return wave // 4, lax.rem(wave // 2, 2), lax.rem(wave, 2), lev // 2, lax.rem(lev, 2)


def at(z, xh, core, y, xl):
    return {"wave": (z * 2 + xh) * 2 + core, "lev": y * 2 + xl}


def lev_peers():
    me = lax.axis_index("lev")
    return [{"lev": lax.rem(me + step, 8)} for step in range(1, 8)]


def greet(peers):
    barrier = pltpu.get_barrier_semaphore()
    for peer in peers:
        pl.semaphore_signal(barrier, inc=1, device_id=peer, device_id_type=MESH)


def met(peers):
    pl.semaphore_wait(pltpu.get_barrier_semaphore(), len(peers))


class Exchange:
    def __init__(self, src, dst, send, recv):
        wave, me = lax.axis_index("wave"), lax.axis_index("lev")
        y, xl = me // 2, lax.rem(me, 2)
        self.copies = []
        for n, (dy, dx) in enumerate(((2, 1), (2, 0), (1, 1), (3, 1), (1, 0), (3, 0), (0, 1))):
            to = lax.rem(y + dy, 4) * 2 + lax.rem(xl + dx, 2)
            self.copies.append(pltpu.make_async_remote_copy(
                src_ref=src.at[to], dst_ref=dst.at[me], send_sem=send.at[n], recv_sem=recv.at[n],
                device_id={"wave": wave, "lev": to}, device_id_type=MESH))

    def start(self):
        for c in self.copies:
            c.start()

    def finish(self):
        for c in self.copies:
            c.wait_recv()

    def sent(self):
        for c in self.copies:
            c.wait_send()


def part():
    lev = lax.axis_index("lev")
    o = lax.rem(lev, 2)
    m0 = 5 * (lev // 2) + 2 * o
    return m0, o, lax.axis_index("wave") * 20 + m0


def band_weights(band_filter, band_blocks):
    keep = jnp.zeros((4, 384), F32)
    block_of = lax.broadcasted_iota(jnp.int32, (4, 384), 1) // 32
    for n in range(12):
        keep = jnp.where(block_of == n, band_blocks[:, n:n + 1].astype(F32), keep)
    return band_filter[...] * keep


def first_kernel(spec, vc, lat, band_filter, band_blocks, leg, cov_out, g_out, lp_out,
                 own_ref, side, w, s_in, lbuf, perm, a_cat, lp, s_cat, g,
                 a_send, a_recv, c_send, c_recv, l_sem, o_sem):
    z, xh, core, y, xl = place()
    me = lax.axis_index("lev")
    zu, zd, z2 = lax.rem(z + 1, 4), lax.rem(z + 3, 4), lax.rem(z + 2, 4)
    yu, yd, y2 = lax.rem(y + 1, 4), lax.rem(y + 3, 4), lax.rem(y + 2, 4)
    up, down = (at(to, xh, core, y, xl) for to in (zu, zd))
    cross = at(z, 1 - xh, core, y, 1 - xl)
    yup, ydown = (at(z, xh, core, to, xl) for to in (yu, yd))
    twin = at(z, xh, 1 - core, y, xl)
    peers = lev_peers() + [up, down, cross, twin]
    m0, o, first = part()
    greet(peers)
    lcopy = pltpu.make_async_copy(leg.at[pl.ds(m0, 3)], lbuf, l_sem.at[0])
    lcopy.start()
    pack_cov(vc, side, own_ref)
    w[...] = band_weights(band_filter, band_blocks)

    def block(zz, xx, kk=None):
        return (zz * 2 + xx) * 2 + (core if kk is None else kk)

    own = block(z, xh)
    columns = (z, zd, zu, z2)
    O = [block(c, xh) for c in columns]
    X = [block(c, 1 - xh) for c in columns]
    ids, started = {}, []

    def piece(blk, row, count):
        return cov_out.at[blk, pl.ds(pl.multiple_of(row, 8), count)]

    def send(name, target, blk, row, count, src=None):
        n = ids.setdefault(name, len(ids))
        ref = piece(blk, row, count)
        copy = pltpu.make_async_remote_copy(
            src_ref=ref if src is None else src.at[pl.ds(pl.multiple_of(row, 8), count)], dst_ref=ref,
            send_sem=c_send.at[n], recv_sem=c_recv.at[n], device_id=target, device_id_type=MESH)
        copy.start()
        started.append(copy)

    def arrived(name, blk, row, count):
        n = ids[name]
        ref = piece(blk, row, count)
        pltpu.make_async_remote_copy(
            src_ref=ref, dst_ref=ref, send_sem=c_send.at[n], recv_sem=c_recv.at[n],
            device_id=twin, device_id_type=MESH).wait_recv()

    def quarter(n):
        return DIRECT + QUARTER * n

    swap = Exchange(spec, s_in, a_send, a_recv)

    locals_ = [pltpu.make_async_copy(spec.at[me], s_in.at[me], l_sem.at[1]),
               pltpu.make_async_copy(own_ref, cov_out.at[own], l_sem.at[2])]

    def z_sends(name, blk, row, count, source=None):
        send(name + "u", up, blk, row, count, source)
        send(name + "d", down, blk, row, count, source)

    def z_on(name, blocks, row, count):
        for way, to, blk, first in (("u", up, blocks[1], row), ("d", down, blocks[2], row + count // 2)):
            send(name + "f" + way, to, blk, first, count // 2)

    def z_got(name, blocks, row, count):
        arrived(name + "u", blocks[1], row, count)
        arrived(name + "d", blocks[2], row, count)

    def z_end(name, blocks, row, count):
        arrived(name + "fu", blocks[3], row, count // 2)
        arrived(name + "fd", blocks[3], row + count // 2, count // 2)

    def y_sends(n):
        send(f"yu{n}", yup, X[n], quarter(y), QUARTER)
        send(f"yd{n}", ydown, X[n], quarter(y), QUARTER)

    def y_on(n):
        if n % 2 == 0:
            arrived(f"yu{n}", X[n], quarter(yd), QUARTER)
            send(f"yf{n}", yup, X[n], quarter(yd), QUARTER)
        else:
            arrived(f"yd{n}", X[n], quarter(yu), QUARTER)
            send(f"yf{n}", ydown, X[n], quarter(yu), QUARTER)

    def begin():
        met(peers)
        send("xs", cross, own, quarter(y), QUARTER, own_ref)
        z_sends("D", own, 0, DIRECT, own_ref)
        swap.start()
        send("xD0", cross, own, 0, DIRECT, own_ref)
        for copy in locals_:
            copy.start()

    def step1():
        arrived("xs", X[0], quarter(y), QUARTER)
        z_sends("s", X[0], quarter(y), QUARTER)
        y_sends(0)

    def step2():
        z_got("D", O, 0, DIRECT)
        z_on("D", O, 0, DIRECT)
        send("xD1", cross, O[1], 0, DIRECT)
        send("xD2", cross, O[2], 0, DIRECT)
        z_got("s", X, quarter(y), QUARTER)
        z_on("s", X, quarter(y), QUARTER)
        z_sends("R", own, DIRECT, REST, own_ref)
        send("t0", twin, own, 0, BLOCK, own_ref)
        y_sends(1)
        y_sends(2)

    def step3():
        z_end("D", O, 0, DIRECT)
        send("xD3", cross, O[3], 0, DIRECT)
        z_end("s", X, quarter(y), QUARTER)
        y_sends(3)
        y_on(0)

    def step4():
        y_on(1)
        y_on(2)

    def step5():
        z_got("R", O, DIRECT, REST)
        z_on("R", O, DIRECT, REST)
        send("t1", twin, O[1], 0, BLOCK)
        send("t2", twin, O[2], 0, BLOCK)
        y_on(3)

    def whole(n):
        arrived(f"xD{n}", X[n], 0, DIRECT)
        if n % 2 == 0:
            arrived(f"yd{n}", X[n], quarter(yu), QUARTER)
        else:
            arrived(f"yu{n}", X[n], quarter(yd), QUARTER)
        arrived(f"yf{n}", X[n], quarter(y2), QUARTER)
        send(f"v{n}", twin, X[n], 0, BLOCK)

    def step9():
        z_end("R", O, DIRECT, REST)
        send("t3", twin, O[3], 0, BLOCK)

    outs = []

    def out(src, dst, n):
        copy = pltpu.make_async_copy(src, dst, o_sem.at[n])
        copy.start()
        outs.append(copy)

    def order():
        for s in range(5):
            g[s, 640:672, :] = jnp.zeros((32, 640), F32)
        row = jnp.broadcast_to(lat[...].reshape(1, 640), (8, 640)).astype(F32)
        column = row.T[:, 0:1]
        mine = row[0:1]
        p_row = lax.broadcasted_iota(jnp.int32, (1, 640), 1)
        rank = jnp.zeros((1, 640), F32)
        for t in range(5):
            c = column[128 * t:128 * t + 128]
            p_col = lax.broadcasted_iota(jnp.int32, (128, 1), 0) + 128 * t
            ahead = (c < mine) | ((c == mine) & (p_col < p_row))
            rank = rank + jnp.sum(ahead.astype(F32), axis=0, keepdims=True)
        for t in range(5):
            place_ = (lax.broadcasted_iota(jnp.int32, (128, 640), 0) + 128 * t).astype(F32)
            perm[128 * t:128 * t + 128, :] = (rank == place_).astype(F32).astype(BF)

    def prep_a(mi):
        hi, lo = split(lbuf[mi])
        p = perm[...]
        ahi = dot_nt(p, hi).astype(BF)
        a_cat[mi, :, 0:384] = ahi
        a_cat[mi, :, 384:768] = ahi
        a_cat[mi, :, 768:1152] = dot_nt(p, lo).astype(BF)

    def prep_b(mi):
        hi, lo = split(lbuf[mi])
        p = perm[...]
        lp[mi, :, 0:640] = dot_nt(hi, p).astype(BF)
        lp[mi, :, 640:1280] = dot_nt(lo, p).astype(BF)
        out(lp.at[mi], lp_out.at[mi], mi)

    def synth(s):
        mi = (s + o) // 2
        tri = (lax.broadcasted_iota(jnp.int32, (1, 384), 1) >= first + mi).astype(F32)
        full = jnp.concatenate([s_in[j, 17 * s:17 * s + 17, :] for j in range(8)], axis=0)
        for b in range(4):
            hi, lo = split(full[0:128] * (w[b:b + 1, :] * tri))
            s_cat[128 * b:128 * (b + 1), 0:384] = hi
            s_cat[128 * b:128 * (b + 1), 384:768] = lo
            s_cat[128 * b:128 * (b + 1), 768:1152] = hi
        tails = jnp.concatenate([full[128:136] * (w[b:b + 1, :] * tri) for b in range(4)], axis=0)
        tails = jnp.concatenate([tails, tails, tails, jnp.zeros_like(tails)], axis=0)
        hi, lo = split(tails)
        s_cat[512:640, 0:384] = hi
        s_cat[512:640, 384:768] = lo
        s_cat[512:640, 768:1152] = hi

        def body(t, _):
            off = pl.multiple_of(t * 256, 256)
            g[s, 0:640, pl.ds(off, 256)] = dot_nt(a_cat[mi], s_cat[pl.ds(off, 256), :])
            return 0

        lax.fori_loop(0, 2, body, 0)
        g[s, 0:640, 512:640] = dot_nt(a_cat[mi], s_cat[512:640, :])
        out(g.at[s], g_out.at[s], 3 + s)

    begin()
    order()
    step1()
    lcopy.wait()
    prep_a(0)
    prep_a(1)
    step2()
    prep_a(2)
    prep_b(0)
    step3()
    prep_b(1)
    prep_b(2)
    step4()
    locals_[0].wait()
    swap.finish()
    synth(0)
    step5()
    synth(1)
    synth(2)
    synth(3)
    step9()
    whole(0)
    whole(1)
    synth(4)
    whole(2)
    whole(3)
    locals_[1].wait()
    swap.sent()
    for copy in outs:
        copy.wait()
    for n in range(4):
        arrived(f"t{n}", block(columns[n], xh, 1 - core), 0, BLOCK)
        arrived(f"v{n}", block(columns[n], 1 - xh, 1 - core), 0, BLOCK)
    for copy in started:
        copy.wait_send()


def first(spec, vc, lat, band_filter, band_blocks, leg):
    hbm = pl.BlockSpec(memory_space=pl.ANY)
    vm = pl.BlockSpec(memory_space=pltpu.VMEM)
    dma = pltpu.SemaphoreType.DMA
    return pl.pallas_call(
        first_kernel,
        out_shape=(jax.ShapeDtypeStruct((16, BLOCK, 128), F32), jax.ShapeDtypeStruct((5, 672, 640), F32),
                   jax.ShapeDtypeStruct((3, 384, 1280), BF)),
        in_specs=[hbm, vm, vm, vm, vm, hbm],
        out_specs=(hbm, hbm, hbm),
        scratch_shapes=[
            pltpu.VMEM((BLOCK, 128), F32),
            pltpu.VMEM((136, 128), F32),
            pltpu.VMEM((4, 384), F32),
            pltpu.VMEM((8, 85, 384), F32),
            pltpu.VMEM((3, 384, 640), F32),
            pltpu.VMEM((640, 640), BF),
            pltpu.VMEM((3, 640, 1152), BF),
            pltpu.VMEM((3, 384, 1280), BF),
            pltpu.VMEM((640, 1152), BF),
            pltpu.VMEM((5, 672, 640), F32),
            dma((7,)), dma((7,)), dma((38,)), dma((38,)), dma((3,)), dma((8,)),
        ],
        compiler_params=pltpu.CompilerParams(collective_id=0, has_side_effects=True, vmem_limit_bytes=58 * 2**20),
    )(spec, vc, lat, band_filter, band_blocks, leg)


def second_kernel(starts, band_filter, band_blocks, g_hbm, lp_hbm, cov_hbm, out_ref, cov, lp_cat, g, cv, wcol, gsem, lsem, csem):
    m0, o, first_m = part()
    gcopies = [pltpu.make_async_copy(g_hbm.at[s], g.at[s], gsem.at[s]) for s in range(5)]
    for copy in gcopies:
        copy.start()

    def cov_copy(n):
        return pltpu.make_async_copy(cov_hbm.at[n], cov.at[n], csem.at[n])

    def begin(n, _):
        cov_copy(n).start()
        return 0

    lax.fori_loop(0, 2, begin, 0)
    lcopies = [pltpu.make_async_copy(lp_hbm.at[:, :, pl.ds(src, 640)], lp_cat.at[:, :, pl.ds(dst, 640)], lsem.at[n])
               for n, (src, dst) in enumerate(((0, 0), (0, 640), (640, 1280)))]
    w = band_weights(band_filter, band_blocks)
    wt = jnp.concatenate([w, w], axis=0).T
    for b in range(4):
        wcol[:, 128 * b:128 * (b + 1)] = jnp.broadcast_to(wt[:, b:b + 1], (384, 128))
    lane = lax.broadcasted_iota(jnp.int32, (384, 128), 1)
    wtail = jnp.zeros((384, 128), F32)
    for b in range(4):
        wtail = jnp.where((lane >= 8 * b) & (lane < 8 * b + 8), wcol[:, 128 * b:128 * (b + 1)], wtail)
    wcol[:, 512:640] = wtail
    for s in range(5):
        cv[s, :, 512:640] = jnp.zeros((672, 128), F32)
    for copy in gcopies:
        copy.wait()
    lax.fori_loop(2, 16, begin, 0)
    for copy in lcopies:
        copy.start()

    lane128 = lax.broadcasted_iota(jnp.int32, (1, 128), 1)
    lane32 = lax.broadcasted_iota(jnp.int32, (1, 32), 1)

    def side(c, blk, odd):
        u = cov[blk, 1088:1224, :]
        u = jnp.where(lax.rem(lane128 // 32, 2) == odd, u, pltpu.roll(u, 32, 1))
        u = jnp.concatenate([u[0:128], u[128:136], u[128:136], u[128:136], u[128:136]], axis=0)
        uhi, ulo = split(u)
        return jnp.where(lane128 < 64, uhi.astype(F32), ulo.astype(F32))

    def window(c, blk, odd, ucat, r0, lo_row, hi_row):
        top = HALF_BLOCK * odd
        trow = cov[blk, top + 512:top + 544, :]
        x = jnp.concatenate([g[s, pl.ds(r0, 32), :] for s in range(5)], axis=0)
        xhi, xlo = split(x)
        t_hi, t_lo = xhi[:, 512:640].astype(F32), xlo[:, 512:640].astype(F32)
        tcat = jnp.where((lane128 >= 32) & (lane128 < 64), t_lo, t_hi).astype(BF)
        row = r0 + lax.broadcasted_iota(jnp.int32, (32, 1), 0)
        keep = (row >= lo_row) & (row < hi_row)
        tail_out = jnp.zeros((160, 32), F32)
        made = []
        for b in range(4):
            of_b = (lax.rem(lane128, 32) >= 8 * b) & (lax.rem(lane128, 32) < 8 * b + 8)
            ub = jnp.where(of_b, ucat, 0.0).astype(BF)
            chi, clo = split(jnp.concatenate([cov[blk, top + 128 * b:top + 128 * b + 128, :], trow], axis=0))
            xb = xhi[:, 128 * b:128 * b + 128]
            lhs = jnp.concatenate([xb, xlo[:, 128 * b:128 * b + 128], xb, tcat], axis=1)
            rhs = jnp.concatenate([chi, chi, clo, ub], axis=1)
            res = dot_nt(lhs, rhs)
            made.append(res[:, 0:128])
            tail_out = jnp.where((lane32 >= 8 * b) & (lane32 < 8 * b + 8), res[:, 128:160], tail_out)
        return r0, keep, made, tail_out

    def put(r0, keep, made, tail_out):
        for s in range(5):
            for b in range(4):
                old = cv[s, pl.ds(r0, 32), 128 * b:128 * b + 128]
                cv[s, pl.ds(r0, 32), 128 * b:128 * b + 128] = jnp.where(keep, made[b][32 * s:32 * s + 32], old)
            old = cv[s, pl.ds(r0, 32), 512:544]
            cv[s, pl.ds(r0, 32), 512:544] = jnp.where(keep, tail_out[32 * s:32 * s + 32], old)

    def covary(blk, _):
        cov_copy(blk).wait()
        firsts = []
        for odd in range(2):
            c = 2 * blk + odd
            lo_row, hi_row = starts[c], starts[c + 1]
            base = jnp.minimum((lo_row // 8) * 8, 632)
            ucat = side(c, blk, odd)
            firsts.append(window(c, blk, odd, ucat, pl.multiple_of(base, 8), lo_row, hi_row))
        for one in firsts:
            put(*one)
        for odd in range(2):
            c = 2 * blk + odd
            lo_row, hi_row = starts[c], starts[c + 1]
            base = jnp.minimum((lo_row // 8) * 8, 632)

            def more(t, _):
                put(*window(c, blk, odd, side(c, blk, odd), pl.multiple_of(base + 32 * t, 8), lo_row, hi_row))
                return 0

            lax.fori_loop(1, (hi_row - base + 31) // 32, more, 0)
        return 0

    lax.fori_loop(0, 16, covary, 0)
    for copy in lcopies:
        copy.wait()

    for s in range(5):
        mi = (s + o) // 2
        acc = None
        for b, wide in ((0, 256), (256, 256), (512, 128)):
            hi, lo = split(cv[s, 0:640, b:b + wide])
            rhs = jnp.concatenate([hi, lo, hi], axis=0)
            one = jnp.dot(lp_cat[mi], rhs, preferred_element_type=F32)
            one = one * wcol[:, b:b + wide]
            if b < 512:
                one = one[:, 0:128] + one[:, 128:256]
                acc = one if acc is None else acc + one
            else:
                tail = one
        tail = tail + pltpu.roll(tail, 128 - 16, 1)
        tail = tail + pltpu.roll(tail, 128 - 8, 1)
        tri = (lax.broadcasted_iota(jnp.int32, (384, 1), 0) >= first_m + mi).astype(F32)
        res = jnp.concatenate([(acc * tri).T, (tail * tri).T[0:8]], axis=0)
        for j in range(8):
            out_ref[j, 17 * s:17 * s + 17, :] = res[17 * j:17 * j + 17]


def second(starts, band_filter, band_blocks, g, lp, cov):
    hbm = pl.BlockSpec(memory_space=pl.ANY)
    vm = pl.BlockSpec(memory_space=pltpu.VMEM)
    dma = pltpu.SemaphoreType.DMA
    return pl.pallas_call(
        second_kernel,
        out_shape=jax.ShapeDtypeStruct((8, 85, 384), F32),
        in_specs=[pl.BlockSpec(memory_space=pltpu.SMEM), vm, vm, hbm, hbm, hbm],
        out_specs=vm,
        scratch_shapes=[
            pltpu.VMEM((16, BLOCK, 128), F32),
            pltpu.VMEM((3, 384, 1920), BF),
            pltpu.VMEM((5, 672, 640), F32),
            pltpu.VMEM((5, 672, 640), F32),
            pltpu.VMEM((384, 640), F32),
            dma((5,)), dma((3,)), dma((16,)),
        ],
        compiler_params=pltpu.CompilerParams(vmem_limit_bytes=58 * 2**20),
    )(starts, band_filter, band_blocks, g, lp, cov)


def return_kernel(src, out, dst, a_send, a_recv, l_sem):
    me = lax.axis_index("lev")
    peers = lev_peers()
    greet(peers)
    met(peers)
    swap = Exchange(src, dst, a_send, a_recv)
    swap.start()
    own = pltpu.make_async_copy(src.at[me], dst.at[me], l_sem)
    own.start()
    own.wait()
    swap.finish()
    for j in range(8):
        for s in range(5):
            out[5 * j + s] = dst[j, 17 * s:17 * s + 17, :]
    swap.sent()


def give_back(x):
    hbm = pl.BlockSpec(memory_space=pl.ANY)
    vm = pl.BlockSpec(memory_space=pltpu.VMEM)
    dma = pltpu.SemaphoreType.DMA
    return pl.pallas_call(
        return_kernel,
        out_shape=jax.ShapeDtypeStruct((40, 17, 384), F32),
        in_specs=[hbm],
        out_specs=vm,
        scratch_shapes=[pltpu.VMEM(x.shape, F32), dma((7,)), dma((7,)), dma(())],
        compiler_params=pltpu.CompilerParams(collective_id=1, has_side_effects=True),
    )(x)


def local(spectra, band_filter, band_blocks, legendre, vert_cov, lat_cov):
    spec = jnp.transpose(spectra, (0, 2, 1, 3)).reshape(8, 85, 384)
    cov, g, lp = first(spec, vert_cov, lat_cov, band_filter, band_blocks, legendre)
    bounds = jnp.arange(40, dtype=jnp.int32)
    starts = jnp.sum((lat_cov[:, None] < bounds[None, :]).astype(jnp.int32), axis=0)
    back = give_back(second(starts, band_filter, band_blocks, g, lp, cov)).reshape(20, 2, 17, 384)
    return jnp.transpose(back, (0, 2, 1, 3))


def solution(mesh):
    P = jax.sharding.PartitionSpec
    return jax.shard_map(
        local,
        mesh=mesh,
        in_specs=(P("wave", "lev", None, None), P(), P(), P("wave", None, None), P(None, "wave", None, None), P()),
        out_specs=P("wave", "lev", None, None),
        check_vma=False,
    )
```
